256 devices in a mesh: segment: 4 (over x), row: 16 (over z, core), col: 4 (over y).
Axes of the slice: x: 4, y: 4, z: 8, core: 2. Of those that a mesh axis runs over, the one named last changes fastest.
Arguments:
- images: bfloat16 [2, 128, 256, 128], P(None, 'row', 'col'), may hold values from -6 to 6
- cotangent: bfloat16 [2, 128, 256, 128], P(None, 'row', 'col'), may hold values from -6 to 6
- weights: bfloat16 [4, 3, 3, 128, 128], P('segment'), may hold values from -0.1875 to 0.1875
- biases: float32 [4, 128], P('segment'), may hold values from -3 to 3
Outputs:
- segment_outputs: bfloat16 [4, 2, 128, 256, 128], P('segment', None, 'row', 'col')
- segment_grads: bfloat16 [4, 2, 128, 256, 128], P('segment', None, 'row', 'col')
- weight_grads: float32 [4, 3, 3, 128, 128], P('segment')
The draws below stay inside these ranges and needn't reach their ends.
All inputs are finite; a program needn't handle non-finite values.
Results may differ from the reference program's by a relative error of at most 0.02.
The reference program's roundings to bfloat16 on the way count: a program that leaves them out, or rounds other values in their place, can miss the bound.
Values may be sent and summed in bfloat16 or wider, within the bound.
A program may use at most 64 MiB of HBM per device.

```python
import jax
import jax.numpy as jnp
from jax import lax

C = 128
MB = 2
SEGMENTS = 4
HEIGHT = 128
WIDTH = 256


def block_levels(key, shape, shards, smallest, largest):
    def one(dim, shards_of):
        steps = jax.random.uniform(jax.random.fold_in(jax.random.fold_in(key, 6), dim), (shards_of,), jnp.float32, smallest / len(shards), largest / len(shards))
        return jnp.repeat(jnp.exp(steps), shape[dim] // shards_of).reshape((-1,) + (1,) * (len(shape) - dim - 1))

    loudness = one(*shards[0])
    for cut in shards[1:]:
        loudness = loudness * one(*cut)
    return loudness


def noise(rng, shape, scale, most, pieces=(), kind=jnp.bfloat16):
    level = block_levels(rng, shape, pieces, -0.22, 0.18) if pieces else 1.0
    entries = jax.random.normal(rng, shape, jnp.float32) * scale * level
    return jnp.minimum(jnp.maximum(entries, -most), most).astype(kind)


def setup_inputs(seed: int = 0) -> dict:
    streams_of = jax.random.split(jax.random.key(seed), 5)
    images = noise(streams_of[0], (MB, HEIGHT, WIDTH, C), 1.0, 6.0, ((1, 16), (2, 4)))
    cotangent = noise(streams_of[1], (MB, HEIGHT, WIDTH, C), 1.0, 6.0, ((1, 16), (2, 4)))
    weights = noise(streams_of[2], (SEGMENTS, 3, 3, C, C), (9 * C) ** -0.5, 0.1875, ((0, 4),))
    biases = noise(streams_of[3], (SEGMENTS, C), 0.5, 3.0, ((0, 4),), jnp.float32)
    return {"images": images, "cotangent": cotangent, "weights": weights, "biases": biases}


def conv_same(active, kernel):
    height, breadth, channels = active.shape
    padded = jnp.pad(active, ((1, 1), (1, 1), (0, 0)))
    total = jnp.zeros((height * breadth, channels), jnp.float32)
    for tap_row in range(3):
        for tap_col in range(3):
            window = padded[tap_row:tap_row + height, tap_col:tap_col + breadth].reshape(-1, channels)
            total = total + jnp.dot(window, kernel[tap_row, tap_col], preferred_element_type=jnp.float32)
    return total.reshape(height, breadth, channels)

def conv_back(grad_out, kernel):
    height, breadth, channels = grad_out.shape
    padded = jnp.pad(grad_out, ((1, 1), (1, 1), (0, 0)))
    total = jnp.zeros((height * breadth, channels), jnp.float32)
    for tap_row in range(3):
        for tap_col in range(3):
            window = padded[2 - tap_row:2 - tap_row + height, 2 - tap_col:2 - tap_col + breadth].reshape(-1, channels)
            total = total + lax.dot_general(window, kernel[tap_row, tap_col], (((1,), (1,)), ((), ())), preferred_element_type=jnp.float32)
    return total.reshape(height, breadth, channels)

def kernel_terms(active, grad_out):
    height, breadth, channels = active.shape
    padded = jnp.pad(active, ((1, 1), (1, 1), (0, 0)))
    flat_grad = grad_out.reshape(-1, channels)
    taps = []
    for tap_row in range(3):
        for tap_col in range(3):
            window = padded[tap_row:tap_row + height, tap_col:tap_col + breadth].reshape(-1, channels)
            taps.append(lax.dot_general(window, flat_grad, (((0,), (0,)), ((), ())), preferred_element_type=jnp.float32))
    return jnp.stack(taps).reshape(3, 3, channels, channels)

def reference(images, cotangent, weights, biases):
    segment_count = weights.shape[0]
    outputs = [[None] * MB for section in range(segment_count)]
    grads = [[None] * MB for section in range(segment_count)]
    totals = [jnp.zeros((3, 3, C, C), jnp.float32) for section in range(segment_count)]
    for batch in range(MB):
        current = images[batch]
        inputs = []
        for section in range(segment_count):
            inputs.append(current)
            active = jnp.maximum(current, jnp.zeros((), current.dtype))
            branch = conv_same(active, weights[section]) + biases[section]
            current = (current.astype(jnp.float32) + branch).astype(jnp.bfloat16)
            outputs[section][batch] = current
        upstream = cotangent[batch]
        for section in reversed(range(segment_count)):
            before = inputs[section]
            active = jnp.maximum(before, jnp.zeros((), before.dtype))
            totals[section] = totals[section] + kernel_terms(active, upstream)
            spread = conv_back(upstream, weights[section])
            upstream = (upstream.astype(jnp.float32) + jnp.where(before > 0, spread, jnp.zeros((), jnp.float32))).astype(jnp.bfloat16)
            grads[section][batch] = upstream
    norming = 1.0 / jnp.sqrt(jnp.float32(MB * HEIGHT * WIDTH))
    segment_outputs = jnp.stack([jnp.stack(outputs[section]) for section in range(segment_count)])
    segment_grads = jnp.stack([jnp.stack(grads[section]) for section in range(segment_count)])
    weight_grads = jnp.stack(totals) * norming
    return (segment_outputs, segment_grads, weight_grads)
```

```python
import functools
import math

import jax
import jax.numpy as jnp
from jax import lax
from jax.experimental import pallas as pl
from jax.experimental.pallas import tpu as pltpu
from jax.sharding import PartitionSpec as P

MESH = pl.DeviceIdType.MESH
BF = jnp.bfloat16
F32 = jnp.float32
SEG, MB, TAPS = 4, 2, 9
REACH = 6
GREACH = 4
SIDE = 16
PAD = 8
DIRS = ((0, 1), (0, -1), (1, 0), (-1, 0), (1, 1), (1, -1), (-1, 1), (-1, -1))


def body_kernel(
    dims, images, cot, w, b, ox, og, ow,
    xin, gin, wall, ball, aa, xs, gg, gs, gm, wf, wb, oxb, ogb, owb,
    dw, s_core, r_core, d_half, s_col, r_col, s_row, r_row, full,
    ss, rs, ls,
):
    rows, width, chan, nrow, ncol, scale = dims
    nz = nrow // 2
    hi = REACH + rows
    tall = rows + 2 * REACH
    wp = width + 2 * PAD
    half, strip = chan // 2, chan // 2 // ncol
    seg, row, col = lax.axis_index("segment"), lax.axis_index("row"), lax.axis_index("col")
    core, z = lax.rem(row, 2), lax.div(row, 2)
    sib = row + 1 - 2 * core

    counter = [0]

    def fresh():
        counter[0] += 1
        return counter[0] - 1

    def remote(src, dst, dev, i):
        return pltpu.make_async_remote_copy(
            src_ref=src, dst_ref=dst, send_sem=ss.at[i], recv_sem=rs.at[i],
            device_id=dev, device_id_type=MESH,
        )

    mine = [
        pltpu.make_async_copy(images.at[m], xin.at[m, pl.ds(REACH, rows), pl.ds(SIDE, width)], ls.at[m])
        for m in range(MB)
    ]
    mine_g = pltpu.make_async_copy(cot, gin.at[:, pl.ds(GREACH, rows), pl.ds(SIDE, width)], ls.at[2])
    mine_w = pltpu.make_async_copy(w, wall.at[seg], ls.at[3])
    mine_b = pltpu.make_async_copy(b, ball.at[seg], ls.at[4])
    for copy in (*mine, mine_g, mine_w, mine_b):
        copy.start()

    barrier = pltpu.get_barrier_semaphore()

    def greet(s, r, c):
        pl.semaphore_signal(barrier, inc=1, device_id=(s, r, c), device_id_type=MESH)

    def inside(dr, dc):
        ok = jnp.bool_(True)
        if dr:
            ok = ok & (row + dr >= 0) & (row + dr < nrow)
        if dc:
            ok = ok & (col + dc >= 0) & (col + dc < ncol)
        return ok

    for k in range(1, SEG):
        greet(lax.rem(seg + k, SEG), row, col)
    for k in range(1, ncol):
        greet(seg, row, lax.rem(col + k, ncol))
    for k in range(1, nz):
        greet(seg, lax.rem(row + 2 * k, nrow), col)
    met = SEG - 1 + ncol - 1 + nz - 1
    for dr, dc in DIRS:
        if dr:
            pl.when(inside(dr, dc))(functools.partial(greet, seg, row + dr, col + dc))
            met = met + inside(dr, dc).astype(jnp.int32)
    pl.semaphore_wait(barrier, met)

    def edges(source, target, reach):
        copies = []
        src_r = {1: (rows - reach, reach), -1: (0, reach), 0: (0, rows)}
        dst_r = {1: (0, reach), -1: (reach + rows, reach), 0: (reach, rows)}
        src_c = {1: (width - SIDE, SIDE), -1: (0, SIDE), 0: (0, width)}
        dst_c = {1: (0, SIDE), -1: (SIDE + width, SIDE), 0: (SIDE, width)}
        for dr, dc in DIRS:
            copies.append((
                remote(
                    source(pl.ds(*src_r[dr]), pl.ds(*src_c[dc])),
                    target(pl.ds(*dst_r[dr]), pl.ds(*dst_c[dc])),
                    (seg, row + dr, col + dc), fresh(),
                ),
                inside(dr, dc), inside(-dr, -dc),
            ))
        return copies

    def start_edges(copies):
        for copy, to, _ in copies:
            pl.when(to)(copy.start)

    def wait_edges(copies):
        for copy, _, of in copies:
            pl.when(of)(copy.wait_recv)

    x_edges = [
        edges(lambda r, c, m=m: images.at[m, r, c], lambda r, c, m=m: xin.at[m, r, c], REACH)
        for m in range(MB)
    ]
    g_edges = edges(lambda r, c: cot.at[:, r, c], lambda r, c: gin.at[:, r, c], GREACH)

    nxt, prv, far = lax.rem(seg + 1, SEG), lax.rem(seg + SEG - 1, SEG), lax.rem(seg + 2, SEG)
    own_rows = pl.ds(pl.multiple_of(half * core, half), half)
    first_q = pl.ds(pl.multiple_of(half * core, half), half // 2)
    second_q = pl.ds(pl.multiple_of(half * core + half // 2, half // 2), half // 2)
    sib_rows = pl.ds(pl.multiple_of(half * (1 - core), half), half)
    up, down = (nxt, row, col), (prv, row, col)
    beside = (seg, sib, col)
    i_up, i_down = fresh(), fresh()
    w_up = remote(w.at[:, own_rows], wall.at[seg, :, own_rows], up, i_up)
    w_down = remote(w.at[:, own_rows], wall.at[seg, :, own_rows], down, i_down)
    got_prv = remote(w.at[:, own_rows], wall.at[prv, :, own_rows], up, i_up)
    got_nxt = remote(w.at[:, own_rows], wall.at[nxt, :, own_rows], down, i_down)

    def onward(which, part, dev, i):
        return remote(wall.at[which, :, part], wall.at[which, :, part], dev, i)

    i_rup, i_rdown, i_s1, i_s2, i_s3 = fresh(), fresh(), fresh(), fresh(), fresh()
    relay_up, relay_down = onward(prv, first_q, up, i_rup), onward(nxt, second_q, down, i_rdown)
    got_rup, got_rdown = onward(far, first_q, up, i_rup), onward(far, second_q, down, i_rdown)
    share_prv, share_nxt = onward(prv, own_rows, beside, i_s1), onward(nxt, own_rows, beside, i_s2)
    share_far = onward(far, own_rows, beside, i_s3)
    got_s1, got_s2 = onward(prv, sib_rows, beside, i_s1), onward(nxt, sib_rows, beside, i_s2)
    got_s3 = onward(far, sib_rows, beside, i_s3)
    b_out, b_in = [], []
    for k in range(1, SEG):
        i = fresh()
        b_out.append(remote(b, ball.at[seg], (lax.rem(seg + k, SEG), row, col), i))
        b_in.append(remote(b, ball.at[lax.rem(seg + SEG - k, SEG)], (lax.rem(seg + k, SEG), row, col), i))

    w_up.start()
    w_down.start()
    start_edges(x_edges[0])
    for copy in b_out:
        copy.start()
    start_edges(x_edges[1])
    start_edges(g_edges)

    got_prv.wait_recv()
    relay_up.start()
    share_prv.start()
    got_nxt.wait_recv()
    relay_down.start()
    share_nxt.start()

    def pass_far():
        got_rup.wait_recv()
        got_rdown.wait_recv()
        share_far.start()

    pl.when(seg == 2)(pass_far)

    def in_image(first, step, count):
        shape = (count, wp, chan)
        r = row * rows - REACH + first + step * lax.broadcasted_iota(jnp.int32, shape, 0)
        c = col * width - PAD + lax.broadcasted_iota(jnp.int32, shape, 1)
        return (r >= 0) & (r < nrow * rows) & (c >= 0) & (c < ncol * width)

    def trio(value):
        flat = value.reshape(-1, chan)
        n = flat.shape[0]
        return [
            v.astype(BF).reshape(value.shape)
            for v in (pltpu.roll(flat, 1, 0), flat, pltpu.roll(flat, n - 1, 0))
        ]

    def take_in(m):
        v = xin[m].astype(F32)[:, PAD : PAD + wp]
        v = jnp.where(in_image(0, 1, tall), v, 0.0)
        xs[m] = v.astype(BF).reshape(tall // 2, 2, wp, chan)
        for t, part in enumerate(trio(jnp.maximum(v, 0.0))):
            aa[0, m, :, :, :, pl.ds(t * chan, chan)] = part.reshape(tall // 2, 2, wp, chan)

    for m in range(MB):
        mine[m].wait()
        wait_edges(x_edges[m])
        take_in(m)

    def build(k):
        zero = jnp.zeros((3 * chan, chan), BF)
        for a in range(4):
            for h in range(2):
                ok = 0 <= a - h <= 2
                block = wall[k, 3 * (a - h) : 3 * (a - h) + 3].reshape(3 * chan, chan) if ok else zero
                wf[k, pl.ds(a * 3 * chan, 3 * chan), pl.ds(h * chan, chan)] = block
                for t in range(3):
                    p = h + 2 - a
                    tile = wall[k, 3 * p + 2 - t] if 0 <= p <= 2 else zero[:chan]
                    wb[k, pl.ds(h * chan, chan), pl.ds((3 * a + t) * chan, chan)] = tile

    def windows(ref, start, count):
        parts = []
        for a in range(4):
            r = start - 1 + a
            parts.append(ref[r // 2 : r // 2 + count // 2, r % 2].reshape(-1, 3 * chan))
        return jnp.concatenate(parts, axis=1)

    def forward(s, m):
        start, count = (s + 1, tall - 2 * (s + 1)) if s < SEG - 1 else (REACH, rows)
        y = jnp.dot(windows(aa.at[s, m], start, count), wf[s], preferred_element_type=F32)
        for h in range(2):
            i, par = (start + h) // 2, (start + h) % 2
            n = count // 2
            x = xs[m, i : i + n, par].astype(F32)
            x = x + (y[:, h * chan : (h + 1) * chan].reshape(n, wp, chan) + ball[s][None])
            x = jnp.where(in_image(start + h, 2, n), x, 0.0).astype(BF)
            xs[m, i : i + n, par] = x
            if s < SEG - 1:
                for t, part in enumerate(trio(jnp.maximum(x.astype(F32), 0.0))):
                    aa[s + 1, m, i : i + n, par, :, pl.ds(t * chan, chan)] = part

    def block_of(ref, m):
        lo, up_to = REACH // 2, hi // 2
        return ref[m, lo:up_to].reshape(rows, wp, chan).astype(F32)

    x_done = pltpu.make_async_copy(oxb, ox, ls.at[5])
    g_done = pltpu.make_async_copy(ogb, og, ls.at[6])

    def emit_x():
        for m in range(MB):
            oxb[m] = block_of(xs, m)[:, PAD : PAD + width].astype(BF)
        x_done.start()

    def emit_g():
        for m in range(MB):
            ogb[m] = block_of(gs, m)[:, PAD : PAD + width].astype(BF)
        g_done.start()

    mine_w.wait()
    mine_b.wait()
    for copy in b_in:
        copy.wait_recv()
    got_s1.wait_recv()
    got_s2.wait_recv()
    pl.when(seg == 2)(got_s3.wait_recv)
    build(0)
    forward(0, 0)
    pl.when(seg != 2)(pass_far)
    forward(0, 1)
    pl.when(seg == 0)(emit_x)
    pl.when(seg != 2)(got_s3.wait_recv)
    for s in range(1, SEG - 1):
        build(s)
        for m in range(MB):
            forward(s, m)
        pl.when(seg == s)(emit_x)
    build(SEG - 1)

    def last():
        for m in range(MB):
            forward(SEG - 1, m)
        emit_x()

    pl.when(seg == SEG - 1)(last)

    mine_g.wait()
    wait_edges(g_edges)
    edge = REACH - GREACH
    for m in range(MB):
        v = gin[m].astype(F32)[:, PAD : PAD + wp]
        v = jnp.where(in_image(edge, 1, tall - 2 * edge), v, 0.0)
        lo, n = edge // 2, tall // 2 - edge
        gs[m, lo : lo + n] = v.astype(BF).reshape(n, 2, wp, chan)
        for t, part in enumerate(trio(v)):
            gg[1, m, lo : lo + n, :, :, pl.ds(t * chan, chan)] = part.reshape(n, 2, wp, chan)
        nothing = jnp.zeros((2, wp, chan), BF)
        gm[m, 0:2] = nothing
        gm[m, rows + 2 : rows + 4] = nothing

    def keep():
        c = lax.broadcasted_iota(jnp.int32, (rows, wp, chan), 1)
        for m in range(MB):
            v = jnp.where((c >= PAD) & (c < PAD + width), block_of(gs, m), 0.0)
            gm[m, 2 : rows + 2] = v.astype(BF)

    def backward(k, m):
        start, count = REACH - k, rows + 2 * k
        y = lax.dot_general(
            windows(gg.at[k % 2, m], start, count), wb[k], (((1,), (1,)), ((), ())),
            preferred_element_type=F32,
        )
        for h in range(2):
            i, par = (start + h) // 2, (start + h) % 2
            n = count // 2
            on = aa[k, m, i : i + n, par, :, pl.ds(chan, chan)].astype(F32) > 0.0
            g = gs[m, i : i + n, par].astype(F32)
            g = (g + jnp.where(on, y[:, h * chan : (h + 1) * chan].reshape(n, wp, chan), 0.0)).astype(BF)
            gs[m, i : i + n, par] = g
            if k:
                for t, part in enumerate(trio(g.astype(F32))):
                    gg[(k - 1) % 2, m, i : i + n, par, :, pl.ds(t * chan, chan)] = part

    for k in range(SEG - 1, 0, -1):
        pl.when(seg == k)(keep)

        def stage(k=k):
            for m in range(MB):
                backward(k, m)

        pl.when(seg <= k)(stage)
        pl.when(seg == k)(emit_g)
    pl.when(seg == 0)(keep)

    total = None
    for m in range(MB):
        lo, up_to = REACH // 2 - 1, hi // 2 + 1
        act = aa[seg, m, lo:up_to].reshape(rows + 4, wp, 3 * chan)[1 : rows + 3].reshape(-1, 3 * chan)
        grads = jnp.concatenate(
            [gm[m, 1 - p : rows + 3 - p].reshape(-1, chan) for p in (-1, 0, 1)], axis=1
        )
        term = lax.dot_general(act, grads, (((0,), (0,)), ((), ())), preferred_element_type=F32)
        total = term if total is None else total + term
    for p in range(3):
        for q in range(3):
            dw[3 * p + q] = total[q * chan : (q + 1) * chan, p * chan : (p + 1) * chan]

    def exchange(pairs):
        for copy, _ in pairs:
            copy.start()
        return pairs

    def arrived(pairs):
        for _, copy in pairs:
            copy.wait_recv()

    late = []
    s_core[...] = dw[:, sib_rows].astype(BF)
    i = fresh()
    core_sum = exchange([(remote(s_core, r_core, beside, i),) * 2])
    late += core_sum
    pl.when(seg == 0)(lambda: backward(0, 0))
    arrived(core_sum)
    d_half[...] = dw[:, own_rows] + r_core[...].astype(F32)
    s_col[...] = d_half[...].astype(BF)
    my_strip = pl.ds(pl.multiple_of(strip * col, strip), strip)
    col_sum = []
    for k in range(1, ncol):
        to = lax.rem(col + k, ncol)
        copy = remote(
            s_col.at[:, pl.ds(pl.multiple_of(strip * to, strip), strip)], r_col.at[k - 1],
            (seg, row, to), fresh(),
        )
        col_sum.append((copy, copy))
    exchange(col_sum)
    late += col_sum

    def final_g():
        backward(0, 1)
        emit_g()

    pl.when(seg == 0)(final_g)
    arrived(col_sum)
    part = d_half[:, my_strip]
    for k in range(1, ncol):
        part = part + r_col[k - 1].astype(F32)
    part = part.astype(BF)
    share = (TAPS - 1) // nz
    for to in range(nz):
        s_row[to, 0:share] = part[to * share : (to + 1) * share]
        s_row[to, share : share + 1] = part[TAPS - 1 :]
    r_row[z] = s_row[z]
    row_sum = []
    for k in range(1, nz):
        to, of = lax.rem(z + k, nz), lax.rem(z + nz - k, nz)
        dev, i = (seg, 2 * to + core, col), fresh()
        row_sum.append((
            remote(s_row.at[to], r_row.at[z], dev, i), remote(s_row.at[to], r_row.at[of], dev, i)
        ))
    exchange(row_sum)
    late += row_sum
    arrived(row_sum)
    done = r_row[0].astype(F32)
    for k in range(1, nz):
        done = done + r_row[k].astype(F32)
    done = (done * scale).astype(BF)
    place = pl.ds(pl.multiple_of(half * core + strip * col, strip), strip)
    full[pl.ds(z * share, share), place] = done[:share]
    full[TAPS - 1 :, place] = done[share:]

    def spread(part_of):
        return full.at[pl.ds(part_of * share, share), place]

    row_all = []
    for k in range(1, nz):
        to, of = lax.rem(z + k, nz), lax.rem(z + nz - k, nz)
        dev, i = (seg, 2 * to + core, col), fresh()
        row_all.append((remote(spread(z), spread(z), dev, i), remote(spread(z), spread(of), dev, i)))
    exchange(row_all)
    late += row_all
    arrived(row_all)

    def column(c):
        return full.at[:, pl.ds(pl.multiple_of(half * core + strip * c, strip), strip)]

    col_all = []
    for k in range(1, ncol):
        to, of = lax.rem(col + k, ncol), lax.rem(col + ncol - k, ncol)
        dev, i = (seg, row, to), fresh()
        col_all.append((remote(column(col), column(col), dev, i), remote(column(col), column(of), dev, i)))
    exchange(col_all)
    late += col_all
    arrived(col_all)
    i = fresh()
    core_all = exchange([(
        remote(full.at[:, own_rows], full.at[:, own_rows], beside, i),
        remote(full.at[:, own_rows], full.at[:, sib_rows], beside, i),
    )])
    late += core_all
    owb[:, own_rows] = full[:, own_rows].astype(F32)
    out_own = pltpu.make_async_copy(owb.at[:, own_rows], ow.at[:, own_rows], ls.at[7])
    out_own.start()

    for copies in (*x_edges, g_edges):
        for copy, to, _ in copies:
            pl.when(to)(copy.wait_send)
    for copy in (w_up, w_down, relay_up, relay_down, share_prv, share_nxt, share_far, *b_out):
        copy.wait_send()
    arrived(core_all)
    owb[:, sib_rows] = full[:, sib_rows].astype(F32)
    out_sib = pltpu.make_async_copy(owb.at[:, sib_rows], ow.at[:, sib_rows], ls.at[8])
    out_sib.start()
    for copy, _ in late:
        copy.wait_send()
    x_done.wait()
    g_done.wait()
    out_own.wait()
    out_sib.wait()


def body(images, cotangent, weights, biases):
    _, rows, width, chan = images.shape
    nrow, ncol = lax.axis_size("row"), lax.axis_size("col")
    nz = nrow // 2
    scale = 1.0 / math.sqrt(MB * rows * nrow * width * ncol)
    dims = (rows, width, chan, nrow, ncol, scale)
    tall, wp = rows + 2 * REACH, width + 2 * PAD
    wide = width + 2 * SIDE
    half, strip = chan // 2, chan // 2 // ncol
    share = (TAPS - 1) // nz
    vm = pltpu.VMEM
    sems = 8 * 3 + 7 + 3 + 2 + 2 * (ncol - 1) + 2 * (nz - 1)
    anywhere = pl.BlockSpec(memory_space=pl.ANY)
    call = pl.pallas_call(
        functools.partial(body_kernel, dims),
        out_shape=(
            jax.ShapeDtypeStruct(images.shape, BF),
            jax.ShapeDtypeStruct(images.shape, BF),
            jax.ShapeDtypeStruct((TAPS, chan, chan), F32),
        ),
        in_specs=[anywhere] * 4,
        out_specs=(anywhere,) * 3,
        scratch_shapes=[
            vm((MB, tall, wide, chan), BF),
            vm((MB, rows + 2 * GREACH, wide, chan), BF),
            vm((SEG, TAPS, chan, chan), BF),
            vm((SEG, 1, chan), F32),
            vm((SEG, MB, tall // 2, 2, wp, 3 * chan), BF),
            vm((MB, tall // 2, 2, wp, chan), BF),
            vm((2, MB, tall // 2, 2, wp, 3 * chan), BF),
            vm((MB, tall // 2, 2, wp, chan), BF),
            vm((MB, rows + 4, wp, chan), BF),
            vm((SEG, 12 * chan, 2 * chan), BF),
            vm((SEG, 2 * chan, 12 * chan), BF),
            vm(images.shape, BF),
            vm(images.shape, BF),
            vm((TAPS, chan, chan), F32),
            vm((TAPS, chan, chan), F32),
            vm((TAPS, half, chan), BF),
            vm((TAPS, half, chan), BF),
            vm((TAPS, half, chan), F32),
            vm((TAPS, half, chan), BF),
            vm((ncol - 1, TAPS, strip, chan), BF),
            vm((nz, share + 1, strip, chan), BF),
            vm((nz, share + 1, strip, chan), BF),
            vm((TAPS, chan, chan), BF),
            pltpu.SemaphoreType.DMA((sems,)),
            pltpu.SemaphoreType.DMA((sems,)),
            pltpu.SemaphoreType.DMA((9,)),
        ],
        compiler_params=pltpu.CompilerParams(
            collective_id=0, has_side_effects=True, vmem_limit_bytes=56 * 2**20
        ),
    )
    outs, grads, kernels = call(
        images, cotangent, weights.reshape(TAPS, chan, chan), biases
    )
    return outs[None], grads[None], kernels.reshape(1, 3, 3, chan, chan)


def solution(mesh):
    placed = (
        P(None, "row", "col", None),
        P(None, "row", "col", None),
        P("segment", None, None, None, None),
        P("segment", None),
    )
    return jax.shard_map(
        body,
        mesh=mesh,
        in_specs=placed,
        out_specs=(
            P("segment", None, "row", "col", None),
            P("segment", None, "row", "col", None),
            P("segment", None, None, None, None),
        ),
        check_vma=False,
    )
```

```python
import functools
import math

import jax
import jax.numpy as jnp
from jax import lax
from jax.experimental import pallas as pl
from jax.experimental.pallas import tpu as pltpu
from jax.sharding import PartitionSpec as P

MESH = pl.DeviceIdType.MESH
BF = jnp.bfloat16
F32 = jnp.float32
SEG, MB, TAPS = 4, 2, 9
REACH = 6
GREACH = 4
WORDS = 5
SIDE = 16
PAD = 8
DIRS = ((0, 1), (0, -1), (1, 0), (-1, 0), (1, 1), (1, -1), (-1, 1), (-1, -1))


def body_kernel(
    dims, images, cot, w, b, ox, og, full,
    xin, gin, wall, ball, aa, xs, gg, gs, gm, wf, wb,
    dw, s_core, r_core, d_half, r_main, r_extra,
    ss, rs, ls, words,
):
    rows, width, chan, nrow, ncol, scale = dims
    nz = nrow // 2
    hi = REACH + rows
    tall = rows + 2 * REACH
    wp = width + 2 * PAD
    half, strip = chan // 2, chan // 2 // ncol
    seg, row, col = lax.axis_index("segment"), lax.axis_index("row"), lax.axis_index("col")
    core, z = lax.rem(row, 2), lax.div(row, 2)
    sib = row + 1 - 2 * core

    def both(step):
        lax.fori_loop(0, MB, lambda m, carry: (step(m), carry)[1], 0)

    counter = [0]

    def fresh():
        counter[0] += 1
        return counter[0] - 1

    def remote(src, dst, dev, i, j=None):
        return pltpu.make_async_remote_copy(
            src_ref=src, dst_ref=dst, send_sem=ss.at[i], recv_sem=rs.at[i if j is None else j],
            device_id=dev, device_id_type=MESH,
        )

    mine = [
        pltpu.make_async_copy(images.at[m], xin.at[m, pl.ds(REACH, rows), pl.ds(SIDE, width)], ls.at[m])
        for m in range(MB)
    ]
    mine_g = pltpu.make_async_copy(cot, gin.at[:, pl.ds(GREACH, rows), pl.ds(SIDE, width)], ls.at[2])
    mine_w = pltpu.make_async_copy(w, wall.at[seg], ls.at[3])
    mine_b = pltpu.make_async_copy(b, ball.at[seg], ls.at[4])
    for copy in (*mine, mine_g, mine_w, mine_b):
        copy.start()

    barrier = pltpu.get_barrier_semaphore()

    def greet(s, r, c):
        pl.semaphore_signal(barrier, inc=1, device_id=(s, r, c), device_id_type=MESH)

    def inside(dr, dc):
        ok = jnp.bool_(True)
        if dr:
            ok = ok & (row + dr >= 0) & (row + dr < nrow)
        if dc:
            ok = ok & (col + dc >= 0) & (col + dc < ncol)
        return ok

    for k in range(1, SEG):
        greet(lax.rem(seg + k, SEG), row, col)
    beside_z = [lax.rem(row + 2, nrow), lax.rem(row + nrow - 2, nrow)]
    beside_y = [lax.rem(col + 1, ncol), lax.rem(col + ncol - 1, ncol)]
    for r in beside_z:
        greet(seg, r, col)
    for c in beside_y:
        greet(seg, row, c)
    met = SEG - 1 + 4
    for dr, dc in DIRS:
        if dr:
            pl.when(inside(dr, dc))(functools.partial(greet, seg, row + dr, col + dc))
            met = met + inside(dr, dc).astype(jnp.int32)
    pl.semaphore_wait(barrier, met)

    def pass_word(n):
        if n:
            pl.semaphore_wait(words.at[n - 1], 2)
        if n < nz // 2 - 1:
            for r in beside_z:
                pl.semaphore_signal(words.at[n], inc=1, device_id=(seg, r, col), device_id_type=MESH)
        elif n < WORDS:
            for c in beside_y:
                pl.semaphore_signal(words.at[n], inc=1, device_id=(seg, row, c), device_id_type=MESH)

    pass_word(0)

    def edges(source, target, reach):
        copies = []
        src_r = {1: (rows - reach, reach), -1: (0, reach), 0: (0, rows)}
        dst_r = {1: (0, reach), -1: (reach + rows, reach), 0: (reach, rows)}
        src_c = {1: (width - SIDE, SIDE), -1: (0, SIDE), 0: (0, width)}
        dst_c = {1: (0, SIDE), -1: (SIDE + width, SIDE), 0: (SIDE, width)}
        for dr, dc in DIRS:
            copies.append((
                remote(
                    source(pl.ds(*src_r[dr]), pl.ds(*src_c[dc])),
                    target(pl.ds(*dst_r[dr]), pl.ds(*dst_c[dc])),
                    (seg, row + dr, col + dc), fresh(),
                ),
                inside(dr, dc), inside(-dr, -dc),
            ))
        return copies

    def start_edges(copies):
        for copy, to, _ in copies:
            pl.when(to)(copy.start)

    def wait_edges(copies):
        for copy, _, of in copies:
            pl.when(of)(copy.wait_recv)

    x_edges = [
        edges(lambda r, c, m=m: images.at[m, r, c], lambda r, c, m=m: xin.at[m, r, c], REACH)
        for m in range(MB)
    ]
    g_edges = edges(lambda r, c: cot.at[:, r, c], lambda r, c: gin.at[:, r, c], GREACH)

    nxt, prv, far = lax.rem(seg + 1, SEG), lax.rem(seg + SEG - 1, SEG), lax.rem(seg + 2, SEG)
    own_rows = pl.ds(pl.multiple_of(half * core, half), half)
    first_q = pl.ds(pl.multiple_of(half * core, half), half // 2)
    second_q = pl.ds(pl.multiple_of(half * core + half // 2, half // 2), half // 2)
    sib_rows = pl.ds(pl.multiple_of(half * (1 - core), half), half)
    up, down = (nxt, row, col), (prv, row, col)
    beside = (seg, sib, col)
    i_ups, i_downs = (fresh(), fresh()), (fresh(), fresh())

    def outward(part, dev, i):
        return remote(w.at[:, part], wall.at[seg, :, part], dev, i)

    def onward(which, part, dev, i):
        return remote(wall.at[which, :, part], wall.at[which, :, part], dev, i)

    w_out = [
        outward(first_q, up, i_ups[0]), outward(second_q, down, i_downs[0]),
        outward(second_q, up, i_ups[1]), outward(first_q, down, i_downs[1]),
    ]
    got_prv = [onward(prv, first_q, up, i_ups[0]), onward(prv, second_q, up, i_ups[1])]
    got_nxt = [onward(nxt, second_q, down, i_downs[0]), onward(nxt, first_q, down, i_downs[1])]
    i_rup, i_rdown, i_s1, i_s2, i_s3 = fresh(), fresh(), fresh(), fresh(), fresh()
    relay_up, relay_down = onward(prv, first_q, up, i_rup), onward(nxt, second_q, down, i_rdown)
    got_rup, got_rdown = onward(far, first_q, up, i_rup), onward(far, second_q, down, i_rdown)
    share_prv, share_nxt = onward(prv, own_rows, beside, i_s1), onward(nxt, own_rows, beside, i_s2)
    share_far = onward(far, own_rows, beside, i_s3)
    got_s1, got_s2 = onward(prv, sib_rows, beside, i_s1), onward(nxt, sib_rows, beside, i_s2)
    got_s3 = onward(far, sib_rows, beside, i_s3)
    b_out, b_in = [], []
    for k in range(1, SEG):
        i = fresh()
        b_out.append(remote(b, ball.at[seg], (lax.rem(seg + k, SEG), row, col), i))
        b_in.append(remote(b, ball.at[lax.rem(seg + SEG - k, SEG)], (lax.rem(seg + k, SEG), row, col), i))

    start_edges(x_edges[0])
    for copy in w_out:
        copy.start()
    start_edges(x_edges[1])
    for copy in b_out:
        copy.start()
    start_edges(g_edges)

    def pass_near():
        got_prv[0].wait_recv()
        relay_up.start()
        got_nxt[0].wait_recv()
        relay_down.start()
        got_prv[1].wait_recv()
        share_prv.start()
        got_nxt[1].wait_recv()
        share_nxt.start()

    def pass_far():
        got_rup.wait_recv()
        got_rdown.wait_recv()
        share_far.start()

    def need(k):
        pl.when(seg == k)(mine_w.wait)
        pl.when(nxt == k)(got_s2.wait_recv)
        pl.when(far == k)(got_s3.wait_recv)
        pl.when(prv == k)(got_s1.wait_recv)

    def in_image(first, step, count):
        shape = (count, wp, chan)
        r = row * rows - REACH + first + step * lax.broadcasted_iota(jnp.int32, shape, 0)
        c = col * width - PAD + lax.broadcasted_iota(jnp.int32, shape, 1)
        return (r >= 0) & (r < nrow * rows) & (c >= 0) & (c < ncol * width)

    def trio(value):
        flat = value.reshape(-1, chan)
        n = flat.shape[0]
        return [
            v.astype(BF).reshape(value.shape)
            for v in (pltpu.roll(flat, 1, 0), flat, pltpu.roll(flat, n - 1, 0))
        ]

    def take_in(m):
        v = xin[m].astype(F32)[:, PAD : PAD + wp]
        v = jnp.where(in_image(0, 1, tall), v, 0.0)
        xs[m] = v.astype(BF).reshape(tall // 2, 2, wp, chan)
        for t, part in enumerate(trio(jnp.maximum(v, 0.0))):
            aa[0, m, :, :, :, pl.ds(t * chan, chan)] = part.reshape(tall // 2, 2, wp, chan)

    def wait_in(m):
        mine[m].wait()
        wait_edges(x_edges[m])

    def build(k):
        zero = jnp.zeros((3 * chan, chan), BF)
        for a in range(4):
            for h in range(2):
                ok = 0 <= a - h <= 2
                block = wall[k, 3 * (a - h) : 3 * (a - h) + 3].reshape(3 * chan, chan) if ok else zero
                wf[k, pl.ds(a * 3 * chan, 3 * chan), pl.ds(h * chan, chan)] = block
                for t in range(3):
                    p = h + 2 - a
                    tile = wall[k, 3 * p + 2 - t] if 0 <= p <= 2 else zero[:chan]
                    wb[k, pl.ds(h * chan, chan), pl.ds((3 * a + t) * chan, chan)] = tile

    def windows(ref, start, count):
        parts = []
        for a in range(4):
            r = start - 1 + a
            parts.append(ref[r // 2 : r // 2 + count // 2, r % 2].reshape(-1, 3 * chan))
        return jnp.concatenate(parts, axis=1)

    def forward(s, m):
        start, count = (s + 1, tall - 2 * (s + 1)) if s < SEG - 1 else (REACH, rows)
        y = jnp.dot(windows(aa.at[s, m], start, count), wf[s], preferred_element_type=F32)
        for h in range(2):
            i, par = (start + h) // 2, (start + h) % 2
            n = count // 2
            x = xs[m, i : i + n, par].astype(F32)
            x = x + (y[:, h * chan : (h + 1) * chan].reshape(n, wp, chan) + ball[s][None])
            x = jnp.where(in_image(start + h, 2, n), x, 0.0).astype(BF)
            xs[m, i : i + n, par] = x
            if s < SEG - 1:
                for t, part in enumerate(trio(jnp.maximum(x.astype(F32), 0.0))):
                    aa[s + 1, m, i : i + n, par, :, pl.ds(t * chan, chan)] = part

    def block_of(ref, m):
        lo, up_to = REACH // 2, hi // 2
        return ref[m, lo:up_to].reshape(rows, wp, chan).astype(F32)

    def emit_x():
        def one(m):
            ox[m] = block_of(xs, m)[:, PAD : PAD + width].astype(BF)

        both(one)

    def emit_g():
        def one(m):
            og[m] = block_of(gs, m)[:, PAD : PAD + width].astype(BF)

        both(one)

    wait_in(0)
    pass_near()
    pl.when(seg == 2)(pass_far)
    need(0)
    mine_b.wait()
    for copy in b_in:
        copy.wait_recv()
    build(0)
    wait_in(1)
    both(take_in)
    both(lambda m: forward(0, m))
    pass_word(1)
    pl.when(seg == 3)(pass_far)
    pl.when(seg == 0)(emit_x)
    need(1)
    build(1)
    both(lambda m: forward(1, m))
    pass_word(2)
    pl.when(seg < 2)(pass_far)
    pl.when(seg == 1)(emit_x)
    need(2)
    build(2)
    both(lambda m: forward(2, m))
    pass_word(3)
    pl.when(seg == 2)(emit_x)
    need(3)
    build(3)

    mine_g.wait()
    wait_edges(g_edges)
    edge = REACH - GREACH
    def take_in_grad(m):
        v = gin[m].astype(F32)[:, PAD : PAD + wp]
        v = jnp.where(in_image(edge, 1, tall - 2 * edge), v, 0.0)
        lo, n = edge // 2, tall // 2 - edge
        gs[m, lo : lo + n] = v.astype(BF).reshape(n, 2, wp, chan)
        for t, part in enumerate(trio(v)):
            gg[1, m, lo : lo + n, :, :, pl.ds(t * chan, chan)] = part.reshape(n, 2, wp, chan)
        nothing = jnp.zeros((2, wp, chan), BF)
        gm[m, 0:2] = nothing
        gm[m, rows + 2 : rows + 4] = nothing

    both(take_in_grad)

    def keep():
        c = lax.broadcasted_iota(jnp.int32, (rows, wp, chan), 1)
        def one(m):
            v = jnp.where((c >= PAD) & (c < PAD + width), block_of(gs, m), 0.0)
            gm[m, 2 : rows + 2] = v.astype(BF)

        both(one)

    def backward(k, m, slot, start, count, more):
        y = lax.dot_general(
            windows(gg.at[slot, m], start, count), wb[k], (((1,), (1,)), ((), ())),
            preferred_element_type=F32,
        )
        for h in range(2):
            i, par = (start + h) // 2, (start + h) % 2
            n = count // 2
            on = aa[k, m, i : i + n, par, :, pl.ds(chan, chan)].astype(F32) > 0.0
            g = gs[m, i : i + n, par].astype(F32)
            g = (g + jnp.where(on, y[:, h * chan : (h + 1) * chan].reshape(n, wp, chan), 0.0)).astype(BF)
            gs[m, i : i + n, par] = g
            if more:
                for t, part in enumerate(trio(g.astype(F32))):
                    gg[1 - slot, m, i : i + n, par, :, pl.ds(t * chan, chan)] = part

    for k in range(SEG - 1, 0, -1):

        def stage(k=k):
            both(lambda m: backward(k, m, k % 2, REACH - k, rows + 2 * k, True))

        pl.when(seg < k)(stage)
        if k == SEG - 1:
            pass_word(4)
    keep()

    def own_grad(m):
        backward(seg, m, lax.rem(seg, 2), REACH, rows, False)

    def last_x():
        both(lambda m: forward(SEG - 1, m))
        emit_x()

    total = None
    for m in range(MB):
        lo, up_to = REACH // 2 - 1, hi // 2 + 1
        act = aa[seg, m, lo:up_to].reshape(rows + 4, wp, 3 * chan)[1 : rows + 3].reshape(-1, 3 * chan)
        grads = jnp.concatenate(
            [gm[m, 1 - p : rows + 3 - p].reshape(-1, chan) for p in (-1, 0, 1)], axis=1
        )
        term = lax.dot_general(act, grads, (((0,), (0,)), ((), ())), preferred_element_type=F32)
        total = term if total is None else total + term
    for p in range(3):
        for q in range(3):
            dw[3 * p + q] = total[q * chan : (q + 1) * chan, p * chan : (p + 1) * chan]

    def exchange(pairs):
        for copy, _ in pairs:
            copy.start()
        return pairs

    def arrived(pairs):
        for _, copy in pairs:
            copy.wait_recv()

    pass_word(5)
    s_core[...] = dw[:, sib_rows].astype(BF)
    i = fresh()
    core_sum = remote(s_core, r_core, beside, i)
    core_sum.start()
    own_grad(0)
    core_sum.wait_recv()
    d_half[...] = (dw[:, own_rows] + r_core[...].astype(F32)).astype(BF)

    share = (TAPS - 1) // nz
    here = col * nz + z
    steps = [(ky, kz) for ky in range(ncol) for kz in range(nz) if ky or kz]

    def strip_of(c):
        return pl.ds(pl.multiple_of(strip * c, strip), strip)

    def place_of(c):
        return pl.ds(pl.multiple_of(half * core + strip * c, strip), strip)

    def taps_of(r):
        return pl.ds(r * share, share)

    def owner(c):
        return c * nz // ncol

    def peer(ky, kz, sign):
        return lax.rem(col + ncol + sign * ky, ncol), lax.rem(z + nz + sign * kz, nz)

    sums = []
    for ky, kz in steps:
        (c, r), (oc, orow) = peer(ky, kz, 1), peer(ky, kz, -1)
        i = fresh()
        src = d_half.at[taps_of(r), strip_of(c)]
        dev = (seg, 2 * r + core, c)
        sums.append((remote(src, r_main.at[here], dev, i), remote(src, r_main.at[oc * nz + orow], dev, i)))
    base_send, base_recv = counter[0], counter[0] + ncol
    counter[0] += ncol + nz * ncol
    extra_out, extra_in = [], []
    last_tap = pl.ds(TAPS - 1, 1)
    for ky in range(ncol):
        c = lax.rem(col + ky, ncol)
        r = owner(c)
        at = ky * nz + lax.rem(r - z + nz, nz)
        extra_out.append((
            remote(
                d_half.at[last_tap, strip_of(c)], r_extra.at[here],
                (seg, 2 * r + core, c), base_send + ky, base_recv + at,
            ),
            at > 0,
        ))
    for ky, kz in steps:
        oc, orow = peer(ky, kz, -1)
        extra_in.append(remote(
            d_half.at[last_tap, strip_of(col)], r_extra.at[oc * nz + orow],
            beside, base_send, base_recv + ky * nz + kz,
        ))
    for copy, on in extra_out:
        pl.when(on)(copy.start)
    for copy, _ in sums:
        copy.start()
    r_main[here] = d_half[taps_of(z), strip_of(col)]
    own = z == owner(col)

    def put_extra():
        r_extra[here] = d_half[last_tap, strip_of(col)]

    pl.when(own)(put_extra)
    own_grad(1)
    emit_g()
    pl.when(seg == SEG - 1)(last_x)

    def total_of(ref):
        done = ref[0].astype(F32)
        for k in range(1, ncol * nz):
            done = done + ref[k].astype(F32)
        return (done * scale).astype(BF)

    spread, spread_extra = [], []
    for ky, kz in steps:
        (c, r), (oc, orow) = peer(ky, kz, 1), peer(ky, kz, -1)
        i = fresh()
        src = full.at[taps_of(z), place_of(col)]
        dev = (seg, 2 * r + core, c)
        spread.append((remote(src, src, dev, i), remote(src, full.at[taps_of(orow), place_of(oc)], dev, i)))
    base_send = counter[0]
    base_recv = counter[0] + len(steps)
    counter[0] += len(steps) + ncol
    for n, (ky, kz) in enumerate(steps):
        c, r = peer(ky, kz, 1)
        src = full.at[last_tap, place_of(col)]
        spread_extra.append(
            remote(src, src, (seg, 2 * r + core, c), base_send + n, base_recv + col)
        )
    got_extra = []
    for c in range(ncol):
        src = full.at[last_tap, place_of(c)]
        got_extra.append((
            remote(src, src, beside, base_send, base_recv + c),
            (col != c) | (z != owner(c)),
        ))

    for _, copy in sums:
        copy.wait_recv()
    full[taps_of(z), place_of(col)] = total_of(r_main)
    for copy, _ in spread:
        copy.start()

    def finish_extra():
        for copy in extra_in:
            copy.wait_recv()
        full[last_tap, place_of(col)] = total_of(r_extra)
        for copy in spread_extra:
            copy.start()

    pl.when(own)(finish_extra)

    for copies in (*x_edges, g_edges):
        for copy, to, _ in copies:
            pl.when(to)(copy.wait_send)
    for copy in (*w_out, relay_up, relay_down, share_prv, share_nxt, share_far, *b_out):
        copy.wait_send()
    for copy, _ in sums:
        copy.wait_send()
    for copy, on in extra_out:
        pl.when(on)(copy.wait_send)
    core_sum.wait_send()

    for _, copy in spread:
        copy.wait_recv()
    for copy, on in got_extra:
        pl.when(on)(copy.wait_recv)
    i = fresh()
    core_all = remote(full.at[:, own_rows], full.at[:, own_rows], beside, i)
    core_got = remote(full.at[:, own_rows], full.at[:, sib_rows], beside, i)
    core_all.start()
    for copy, _ in spread:
        copy.wait_send()

    def extra_left():
        for copy in spread_extra:
            copy.wait_send()

    pl.when(own)(extra_left)
    core_got.wait_recv()
    core_all.wait_send()


def write_kernel(x, g, k, ox, og, ow, buf, sems):
    copies = [pltpu.make_async_copy(x, ox, sems.at[0]), pltpu.make_async_copy(g, og, sems.at[1])]
    for copy in copies:
        copy.start()
    buf[...] = k[...].astype(F32)
    copies.append(pltpu.make_async_copy(buf, ow, sems.at[2]))
    copies[-1].start()
    for copy in copies:
        copy.wait()


def body(images, cotangent, weights, biases):
    _, rows, width, chan = images.shape
    nrow, ncol = lax.axis_size("row"), lax.axis_size("col")
    nz = nrow // 2
    scale = 1.0 / math.sqrt(MB * rows * nrow * width * ncol)
    dims = (rows, width, chan, nrow, ncol, scale)
    tall, wp = rows + 2 * REACH, width + 2 * PAD
    wide = width + 2 * SIDE
    half, strip = chan // 2, chan // 2 // ncol
    share = (TAPS - 1) // nz
    vm = pltpu.VMEM
    chips = ncol * nz
    sems = 8 * 3 + 9 + 3 + 2 + 4 * chips + 2 * ncol
    anywhere = pl.BlockSpec(memory_space=pl.ANY)
    inside = pl.BlockSpec(memory_space=pltpu.VMEM)
    call = pl.pallas_call(
        functools.partial(body_kernel, dims),
        out_shape=(vm(images.shape, BF), vm(images.shape, BF), vm((TAPS, chan, chan), BF)),
        in_specs=[anywhere] * 4,
        out_specs=(inside,) * 3,
        scratch_shapes=[
            vm((MB, tall, wide, chan), BF),
            vm((MB, rows + 2 * GREACH, wide, chan), BF),
            vm((SEG, TAPS, chan, chan), BF),
            vm((SEG, 1, chan), F32),
            vm((SEG, MB, tall // 2, 2, wp, 3 * chan), BF),
            vm((MB, tall // 2, 2, wp, chan), BF),
            vm((2, MB, tall // 2, 2, wp, 3 * chan), BF),
            vm((MB, tall // 2, 2, wp, chan), BF),
            vm((MB, rows + 4, wp, chan), BF),
            vm((SEG, 12 * chan, 2 * chan), BF),
            vm((SEG, 2 * chan, 12 * chan), BF),
            vm((TAPS, chan, chan), F32),
            vm((TAPS, half, chan), BF),
            vm((TAPS, half, chan), BF),
            vm((TAPS, half, chan), BF),
            vm((chips, share, strip, chan), BF),
            vm((chips, 1, strip, chan), BF),
            pltpu.SemaphoreType.DMA((sems,)),
            pltpu.SemaphoreType.DMA((sems,)),
            pltpu.SemaphoreType.DMA((5,)),
            pltpu.SemaphoreType.REGULAR((WORDS,)),
        ],
        compiler_params=pltpu.CompilerParams(
            collective_id=0, has_side_effects=True, vmem_limit_bytes=56 * 2**20
        ),
    )
    results = call(images, cotangent, weights.reshape(TAPS, chan, chan), biases)
    outs, grads, kernels = pl.pallas_call(
        write_kernel,
        out_shape=(
            jax.ShapeDtypeStruct(images.shape, BF),
            jax.ShapeDtypeStruct(images.shape, BF),
            jax.ShapeDtypeStruct((TAPS, chan, chan), F32),
        ),
        in_specs=[inside] * 3,
        out_specs=(anywhere,) * 3,
        scratch_shapes=[vm((TAPS, chan, chan), F32), pltpu.SemaphoreType.DMA((3,))],
        compiler_params=pltpu.CompilerParams(vmem_limit_bytes=4 * 2**20),
    )(*results)
    return outs[None], grads[None], kernels.reshape(1, 3, 3, chan, chan)


def solution(mesh):
    placed = (
        P(None, "row", "col", None),
        P(None, "row", "col", None),
        P("segment", None, None, None, None),
        P("segment", None),
    )
    return jax.shard_map(
        body,
        mesh=mesh,
        in_specs=placed,
        out_specs=(
            P("segment", None, "row", "col", None),
            P("segment", None, "row", "col", None),
            P("segment", None, None, None, None),
        ),
        check_vma=False,
    )
```

```python
import functools
import math

import jax
import jax.numpy as jnp
from jax import lax
from jax.experimental import pallas as pl
from jax.experimental.pallas import tpu as pltpu
from jax.sharding import PartitionSpec as P

MESH = pl.DeviceIdType.MESH
BF = jnp.bfloat16
F32 = jnp.float32
SEG, MB, TAPS = 4, 2, 9
REACH = 6
GREACH = 4
WORDS = 5
SIDE = 16
PAD = 8
DIRS = ((0, 1), (0, -1), (1, 0), (-1, 0), (1, 1), (1, -1), (-1, 1), (-1, -1))


def wrap(v, n):
    return jnp.where(v >= n, v - n, v)


def body_kernel(
    dims, images, cot, w, b, ox, og, full,
    xin, gin, wall, ball, aa, xs, gg, gs, gm, wf, wb,
    dw, s_core, r_core, d_half, r_main, r_tap_col, s_tap, r_tap_row,
    ss, rs, ls, words,
):
    rows, width, chan, nrow, ncol, scale = dims
    nz = nrow // 2
    hi = REACH + rows
    tall = rows + 2 * REACH
    wp = width + 2 * PAD
    half, strip = chan // 2, chan // 2 // ncol
    seg, row, col = lax.axis_index("segment"), lax.axis_index("row"), lax.axis_index("col")
    core, z = lax.rem(row, 2), lax.div(row, 2)
    sib = row + 1 - 2 * core

    def both(step):
        lax.fori_loop(0, MB, lambda m, carry: (step(m), carry)[1], 0)

    counter = [0]

    def fresh():
        counter[0] += 1
        return counter[0] - 1

    def remote(src, dst, dev, i, j=None):
        return pltpu.make_async_remote_copy(
            src_ref=src, dst_ref=dst, send_sem=ss.at[i], recv_sem=rs.at[i if j is None else j],
            device_id=dev, device_id_type=MESH,
        )

    mine = [
        pltpu.make_async_copy(images.at[m], xin.at[m, pl.ds(REACH, rows), pl.ds(SIDE, width)], ls.at[m])
        for m in range(MB)
    ]
    mine_g = pltpu.make_async_copy(cot, gin.at[:, pl.ds(GREACH, rows), pl.ds(SIDE, width)], ls.at[2])
    mine_w = pltpu.make_async_copy(w, wall.at[seg], ls.at[3])
    mine_b = pltpu.make_async_copy(b, ball.at[seg], ls.at[4])
    for copy in (*mine, mine_g, mine_w, mine_b):
        copy.start()

    barrier = pltpu.get_barrier_semaphore()

    def greet(s, r, c):
        pl.semaphore_signal(barrier, inc=1, device_id=(s, r, c), device_id_type=MESH)

    def inside(dr, dc):
        ok = jnp.bool_(True)
        if dr:
            ok = ok & (row + dr >= 0) & (row + dr < nrow)
        if dc:
            ok = ok & (col + dc >= 0) & (col + dc < ncol)
        return ok

    for k in range(1, SEG):
        greet(lax.rem(seg + k, SEG), row, col)
    beside_z = [lax.rem(row + 2, nrow), lax.rem(row + nrow - 2, nrow)]
    beside_y = [lax.rem(col + 1, ncol), lax.rem(col + ncol - 1, ncol)]
    for r in beside_z:
        greet(seg, r, col)
    for c in beside_y:
        greet(seg, row, c)
    met = SEG - 1 + 4
    for dr, dc in DIRS:
        if dr:
            pl.when(inside(dr, dc))(functools.partial(greet, seg, row + dr, col + dc))
            met = met + inside(dr, dc).astype(jnp.int32)
    pl.semaphore_wait(barrier, met)

    def pass_word(n):
        if n:
            pl.semaphore_wait(words.at[n - 1], 2)
        if n < nz // 2 - 1:
            for r in beside_z:
                pl.semaphore_signal(words.at[n], inc=1, device_id=(seg, r, col), device_id_type=MESH)
        elif n < WORDS:
            for c in beside_y:
                pl.semaphore_signal(words.at[n], inc=1, device_id=(seg, row, c), device_id_type=MESH)

    pass_word(0)

    def edges(source, target, reach):
        copies = []
        src_r = {1: (rows - reach, reach), -1: (0, reach), 0: (0, rows)}
        dst_r = {1: (0, reach), -1: (reach + rows, reach), 0: (reach, rows)}
        src_c = {1: (width - SIDE, SIDE), -1: (0, SIDE), 0: (0, width)}
        dst_c = {1: (0, SIDE), -1: (SIDE + width, SIDE), 0: (SIDE, width)}
        for dr, dc in DIRS:
            copies.append((
                remote(
                    source(pl.ds(*src_r[dr]), pl.ds(*src_c[dc])),
                    target(pl.ds(*dst_r[dr]), pl.ds(*dst_c[dc])),
                    (seg, row + dr, col + dc), fresh(),
                ),
                inside(dr, dc), inside(-dr, -dc),
            ))
        return copies

    def start_edges(copies):
        for copy, to, _ in copies:
            pl.when(to)(copy.start)

    def wait_edges(copies):
        for copy, _, of in copies:
            pl.when(of)(copy.wait_recv)

    x_edges = [
        edges(lambda r, c, m=m: images.at[m, r, c], lambda r, c, m=m: xin.at[m, r, c], REACH)
        for m in range(MB)
    ]
    g_edges = edges(lambda r, c: cot.at[:, r, c], lambda r, c: gin.at[:, r, c], GREACH)

    nxt, prv, far = lax.rem(seg + 1, SEG), lax.rem(seg + SEG - 1, SEG), lax.rem(seg + 2, SEG)
    own_rows = pl.ds(pl.multiple_of(half * core, half), half)
    first_q = pl.ds(pl.multiple_of(half * core, half), half // 2)
    second_q = pl.ds(pl.multiple_of(half * core + half // 2, half // 2), half // 2)
    sib_rows = pl.ds(pl.multiple_of(half * (1 - core), half), half)
    up, down = (nxt, row, col), (prv, row, col)
    beside = (seg, sib, col)
    i_ups, i_downs = (fresh(), fresh()), (fresh(), fresh())

    def outward(part, dev, i):
        return remote(w.at[:, part], wall.at[seg, :, part], dev, i)

    def onward(which, part, dev, i):
        return remote(wall.at[which, :, part], wall.at[which, :, part], dev, i)

    w_out = [
        outward(first_q, up, i_ups[0]), outward(second_q, down, i_downs[0]),
        outward(second_q, up, i_ups[1]), outward(first_q, down, i_downs[1]),
    ]
    got_prv = [onward(prv, first_q, up, i_ups[0]), onward(prv, second_q, up, i_ups[1])]
    got_nxt = [onward(nxt, second_q, down, i_downs[0]), onward(nxt, first_q, down, i_downs[1])]
    i_rup, i_rdown, i_s1, i_s2, i_s3 = fresh(), fresh(), fresh(), fresh(), fresh()
    relay_up, relay_down = onward(prv, first_q, up, i_rup), onward(nxt, second_q, down, i_rdown)
    got_rup, got_rdown = onward(far, first_q, up, i_rup), onward(far, second_q, down, i_rdown)
    share_prv, share_nxt = onward(prv, own_rows, beside, i_s1), onward(nxt, own_rows, beside, i_s2)
    share_far = onward(far, own_rows, beside, i_s3)
    got_s1, got_s2 = onward(prv, sib_rows, beside, i_s1), onward(nxt, sib_rows, beside, i_s2)
    got_s3 = onward(far, sib_rows, beside, i_s3)
    b_out, b_in = [], []
    for k in range(1, SEG):
        i = fresh()
        b_out.append(remote(b, ball.at[seg], (lax.rem(seg + k, SEG), row, col), i))
        b_in.append(remote(b, ball.at[lax.rem(seg + SEG - k, SEG)], (lax.rem(seg + k, SEG), row, col), i))

    start_edges(x_edges[0])
    for copy in w_out:
        copy.start()
    start_edges(x_edges[1])
    for copy in b_out:
        copy.start()
    start_edges(g_edges)

    def pass_near():
        got_prv[0].wait_recv()
        relay_up.start()
        got_nxt[0].wait_recv()
        relay_down.start()
        got_prv[1].wait_recv()
        share_prv.start()
        got_nxt[1].wait_recv()
        share_nxt.start()

    def pass_far():
        got_rup.wait_recv()
        got_rdown.wait_recv()
        share_far.start()

    def need(k):
        pl.when(seg == k)(mine_w.wait)
        pl.when(nxt == k)(got_s2.wait_recv)
        pl.when(far == k)(got_s3.wait_recv)
        pl.when(prv == k)(got_s1.wait_recv)

    def in_image(first, step, count):
        shape = (count, wp, chan)
        r = row * rows - REACH + first + step * lax.broadcasted_iota(jnp.int32, shape, 0)
        c = col * width - PAD + lax.broadcasted_iota(jnp.int32, shape, 1)
        return (r >= 0) & (r < nrow * rows) & (c >= 0) & (c < ncol * width)

    def trio(value):
        flat = value.reshape(-1, chan)
        n = flat.shape[0]
        return [
            v.astype(BF).reshape(value.shape)
            for v in (pltpu.roll(flat, 1, 0), flat, pltpu.roll(flat, n - 1, 0))
        ]

    def take_in(m):
        v = xin[m].astype(F32)[:, PAD : PAD + wp]
        v = jnp.where(in_image(0, 1, tall), v, 0.0)
        xs[m] = v.astype(BF).reshape(tall // 2, 2, wp, chan)
        for t, part in enumerate(trio(jnp.maximum(v, 0.0))):
            aa[0, m, :, :, :, pl.ds(t * chan, chan)] = part.reshape(tall // 2, 2, wp, chan)

    def wait_in(m):
        mine[m].wait()
        wait_edges(x_edges[m])

    def build(k):
        zero = jnp.zeros((3 * chan, chan), BF)
        for a in range(4):
            for h in range(2):
                ok = 0 <= a - h <= 2
                block = wall[k, 3 * (a - h) : 3 * (a - h) + 3].reshape(3 * chan, chan) if ok else zero
                wf[k, pl.ds(a * 3 * chan, 3 * chan), pl.ds(h * chan, chan)] = block
                for t in range(3):
                    p = h + 2 - a
                    tile = wall[k, 3 * p + 2 - t] if 0 <= p <= 2 else zero[:chan]
                    wb[k, pl.ds(h * chan, chan), pl.ds((3 * a + t) * chan, chan)] = tile

    def windows(ref, start, count):
        parts = []
        for a in range(4):
            r = start - 1 + a
            parts.append(ref[r // 2 : r // 2 + count // 2, r % 2].reshape(-1, 3 * chan))
        return jnp.concatenate(parts, axis=1)

    def forward(s, m):
        start, count = (s + 1, tall - 2 * (s + 1)) if s < SEG - 1 else (REACH, rows)
        y = jnp.dot(windows(aa.at[s, m], start, count), wf[s], preferred_element_type=F32)
        for h in range(2):
            i, par = (start + h) // 2, (start + h) % 2
            n = count // 2
            x = xs[m, i : i + n, par].astype(F32)
            x = x + (y[:, h * chan : (h + 1) * chan].reshape(n, wp, chan) + ball[s][None])
            x = jnp.where(in_image(start + h, 2, n), x, 0.0).astype(BF)
            xs[m, i : i + n, par] = x
            if s < SEG - 1:
                for t, part in enumerate(trio(jnp.maximum(x.astype(F32), 0.0))):
                    aa[s + 1, m, i : i + n, par, :, pl.ds(t * chan, chan)] = part

    def block_of(ref, m):
        lo, up_to = REACH // 2, hi // 2
        return ref[m, lo:up_to].reshape(rows, wp, chan).astype(F32)

    def emit_x():
        def one(m):
            ox[m] = block_of(xs, m)[:, PAD : PAD + width].astype(BF)

        both(one)

    def emit_g():
        def one(m):
            og[m] = block_of(gs, m)[:, PAD : PAD + width].astype(BF)

        both(one)

    wait_in(0)
    take_in(0)
    pass_near()
    pass_word(1)
    pl.when(seg == 2)(pass_far)
    need(0)
    mine_b.wait()
    for copy in b_in:
        copy.wait_recv()
    build(0)
    forward(0, 0)
    wait_in(1)
    take_in(1)
    forward(0, 1)
    pass_word(2)
    pl.when(seg == 3)(pass_far)
    pl.when(seg == 0)(emit_x)
    need(1)
    build(1)
    both(lambda m: forward(1, m))
    pass_word(3)
    pl.when(seg < 2)(pass_far)
    pl.when(seg == 1)(emit_x)
    need(2)
    build(2)
    both(lambda m: forward(2, m))
    pass_word(4)
    pl.when(seg == 2)(emit_x)
    need(3)
    build(3)

    mine_g.wait()
    wait_edges(g_edges)
    edge = REACH - GREACH
    def take_in_grad(m):
        v = gin[m].astype(F32)[:, PAD : PAD + wp]
        v = jnp.where(in_image(edge, 1, tall - 2 * edge), v, 0.0)
        lo, n = edge // 2, tall // 2 - edge
        gs[m, lo : lo + n] = v.astype(BF).reshape(n, 2, wp, chan)
        for t, part in enumerate(trio(v)):
            gg[1, m, lo : lo + n, :, :, pl.ds(t * chan, chan)] = part.reshape(n, 2, wp, chan)
        nothing = jnp.zeros((2, wp, chan), BF)
        gm[m, 0:2] = nothing
        gm[m, rows + 2 : rows + 4] = nothing

    both(take_in_grad)

    def keep():
        c = lax.broadcasted_iota(jnp.int32, (rows, wp, chan), 1)
        def one(m):
            v = jnp.where((c >= PAD) & (c < PAD + width), block_of(gs, m), 0.0)
            gm[m, 2 : rows + 2] = v.astype(BF)

        both(one)

    def backward(k, m, slot, start, count, more):
        y = lax.dot_general(
            windows(gg.at[slot, m], start, count), wb[k], (((1,), (1,)), ((), ())),
            preferred_element_type=F32,
        )
        for h in range(2):
            i, par = (start + h) // 2, (start + h) % 2
            n = count // 2
            on = aa[k, m, i : i + n, par, :, pl.ds(chan, chan)].astype(F32) > 0.0
            g = gs[m, i : i + n, par].astype(F32)
            g = (g + jnp.where(on, y[:, h * chan : (h + 1) * chan].reshape(n, wp, chan), 0.0)).astype(BF)
            gs[m, i : i + n, par] = g
            if more:
                for t, part in enumerate(trio(g.astype(F32))):
                    gg[1 - slot, m, i : i + n, par, :, pl.ds(t * chan, chan)] = part

    for k in range(SEG - 1, 0, -1):

        def stage(k=k):
            both(lambda m: backward(k, m, k % 2, REACH - k, rows + 2 * k, True))

        pl.when(seg < k)(stage)
        if k == SEG - 1:
            pass_word(5)
    keep()

    def own_grad(m):
        backward(seg, m, lax.rem(seg, 2), REACH, rows, False)

    def last_x():
        both(lambda m: forward(SEG - 1, m))
        emit_x()

    total = None
    for m in range(MB):
        lo, up_to = REACH // 2 - 1, hi // 2 + 1
        act = aa[seg, m, lo:up_to].reshape(rows + 4, wp, 3 * chan)[1 : rows + 3].reshape(-1, 3 * chan)
        grads = jnp.concatenate(
            [gm[m, 1 - p : rows + 3 - p].reshape(-1, chan) for p in (-1, 0, 1)], axis=1
        )
        term = lax.dot_general(act, grads, (((0,), (0,)), ((), ())), preferred_element_type=F32)
        total = term if total is None else total + term
    for p in range(3):
        for q in range(3):
            dw[3 * p + q] = total[q * chan : (q + 1) * chan, p * chan : (p + 1) * chan]

    def exchange(pairs):
        for copy, _ in pairs:
            copy.start()
        return pairs

    def arrived(pairs):
        for _, copy in pairs:
            copy.wait_recv()

    s_core[...] = dw[:, sib_rows].astype(BF)
    i = fresh()
    core_sum = remote(s_core, r_core, beside, i)
    core_sum.start()
    own_grad(0)
    core_sum.wait_recv()
    d_half[...] = (dw[:, own_rows] + r_core[...].astype(F32)).astype(BF)

    share = (TAPS - 1) // nz
    main = TAPS - 1
    last_tap = pl.ds(main, 1)
    cols = [wrap(col + k, ncol) for k in range(ncol)]
    zs = [wrap(z + k, nz) for k in range(nz)]
    strips = [pl.ds(pl.multiple_of(strip * c, strip), strip) for c in cols]
    places = [pl.ds(pl.multiple_of(half * core + strip * c, strip), strip) for c in cols]
    taps = [pl.ds(r * share, share) for r in zs]
    slots = [[c * nz + r for r in zs] for c in cols]
    steps = [(ky, kz) for ky in range(ncol) for kz in range(nz) if ky or kz]
    steps.sort(key=lambda s: -min(s[0], ncol - s[0]) - min(s[1], nz - s[1]))

    def device(ky, kz):
        return seg, 2 * zs[kz] + core, cols[ky]

    tap_col = [
        remote(d_half.at[last_tap, strips[k]], r_tap_col.at[k - 1], device(k, 0), fresh())
        for k in range(1, ncol)
    ]
    for copy in tap_col:
        copy.start()

    sums = []
    for ky, kz in steps:
        i = fresh()
        src = d_half.at[taps[kz], strips[ky]]
        sums.append((
            remote(src, r_main.at[slots[0][0]], device(ky, kz), i),
            remote(src, r_main.at[slots[-ky % ncol][-kz % nz]], device(ky, kz), i),
        ))
    for copy, _ in sums:
        copy.start()
    r_main[slots[0][0]] = d_half[taps[0], strips[0]]
    own_grad(1)
    emit_g()
    pl.when(seg == SEG - 1)(last_x)

    def total_of(ref, count):
        done = ref[0].astype(F32)
        for k in range(1, count):
            done = done + ref[k].astype(F32)
        return done

    for copy in tap_col:
        copy.wait_recv()
    tap = d_half[last_tap, strips[0]].astype(F32) + total_of(r_tap_col, ncol - 1)
    s_tap[...] = tap.astype(BF)
    r_tap_row[z] = tap.astype(BF)
    tap_row = []
    for k in range(1, nz):
        i = fresh()
        tap_row.append((
            remote(s_tap, r_tap_row.at[z], device(0, k), i),
            remote(s_tap, r_tap_row.at[zs[nz - k]], device(0, k), i),
        ))
    for copy, _ in tap_row:
        copy.start()

    spread = []
    for ky, kz in steps:
        i = fresh()
        src = full.at[taps[0], places[0]]
        spread.append((
            remote(src, src, device(ky, kz), i),
            remote(src, full.at[taps[-kz % nz], places[-ky % ncol]], device(ky, kz), i),
        ))
    for _, copy in sums:
        copy.wait_recv()
    full[taps[0], places[0]] = (total_of(r_main, ncol * nz) * scale).astype(BF)
    for copy, _ in spread:
        copy.start()
    for _, copy in tap_row:
        copy.wait_recv()
    full[last_tap, places[0]] = (total_of(r_tap_row, nz) * scale).astype(BF)
    tap_all = []
    for k in range(1, ncol):
        i = fresh()
        src = full.at[last_tap, places[0]]
        tap_all.append((
            remote(src, src, device(k, 0), i),
            remote(src, full.at[last_tap, places[ncol - k]], device(k, 0), i),
        ))
    for copy, _ in tap_all:
        copy.start()

    for copies in (*x_edges, g_edges):
        for copy, to, _ in copies:
            pl.when(to)(copy.wait_send)
    for copy in (*w_out, relay_up, relay_down, share_prv, share_nxt, share_far, *b_out):
        copy.wait_send()
    for copy, _ in (*sums, *tap_row):
        copy.wait_send()
    for copy in (core_sum, *tap_col):
        copy.wait_send()

    for _, copy in (*spread, *tap_all):
        copy.wait_recv()
    i = fresh()
    core_all = remote(full.at[:, own_rows], full.at[:, own_rows], beside, i)
    core_got = remote(full.at[:, own_rows], full.at[:, sib_rows], beside, i)
    core_all.start()
    for copy, _ in (*spread, *tap_all):
        copy.wait_send()
    core_got.wait_recv()
    core_all.wait_send()


def write_kernel(x, g, k, ox, og, ow, buf, sems):
    copies = [pltpu.make_async_copy(x, ox, sems.at[0]), pltpu.make_async_copy(g, og, sems.at[1])]
    for copy in copies:
        copy.start()
    buf[...] = k[...].astype(F32)
    copies.append(pltpu.make_async_copy(buf, ow, sems.at[2]))
    copies[-1].start()
    for copy in copies:
        copy.wait()


def body(images, cotangent, weights, biases):
    _, rows, width, chan = images.shape
    nrow, ncol = lax.axis_size("row"), lax.axis_size("col")
    nz = nrow // 2
    scale = 1.0 / math.sqrt(MB * rows * nrow * width * ncol)
    dims = (rows, width, chan, nrow, ncol, scale)
    tall, wp = rows + 2 * REACH, width + 2 * PAD
    wide = width + 2 * SIDE
    half, strip = chan // 2, chan // 2 // ncol
    share = (TAPS - 1) // nz
    vm = pltpu.VMEM
    chips = ncol * nz
    sems = 8 * 3 + 9 + 3 + 2 + 2 * (chips - 1) + 2 * (ncol - 1) + nz - 1
    anywhere = pl.BlockSpec(memory_space=pl.ANY)
    inside = pl.BlockSpec(memory_space=pltpu.VMEM)
    call = pl.pallas_call(
        functools.partial(body_kernel, dims),
        out_shape=(vm(images.shape, BF), vm(images.shape, BF), vm((TAPS, chan, chan), BF)),
        in_specs=[anywhere] * 4,
        out_specs=(inside,) * 3,
        scratch_shapes=[
            vm((MB, tall, wide, chan), BF),
            vm((MB, rows + 2 * GREACH, wide, chan), BF),
            vm((SEG, TAPS, chan, chan), BF),
            vm((SEG, 1, chan), F32),
            vm((SEG, MB, tall // 2, 2, wp, 3 * chan), BF),
            vm((MB, tall // 2, 2, wp, chan), BF),
            vm((2, MB, tall // 2, 2, wp, 3 * chan), BF),
            vm((MB, tall // 2, 2, wp, chan), BF),
            vm((MB, rows + 4, wp, chan), BF),
            vm((SEG, 12 * chan, 2 * chan), BF),
            vm((SEG, 2 * chan, 12 * chan), BF),
            vm((TAPS, chan, chan), F32),
            vm((TAPS, half, chan), BF),
            vm((TAPS, half, chan), BF),
            vm((TAPS, half, chan), BF),
            vm((chips, share, strip, chan), BF),
            vm((ncol - 1, 1, strip, chan), BF),
            vm((1, strip, chan), BF),
            vm((nz, 1, strip, chan), BF),
            pltpu.SemaphoreType.DMA((sems,)),
            pltpu.SemaphoreType.DMA((sems,)),
            pltpu.SemaphoreType.DMA((5,)),
            pltpu.SemaphoreType.REGULAR((WORDS,)),
        ],
        compiler_params=pltpu.CompilerParams(
            collective_id=0, has_side_effects=True, vmem_limit_bytes=56 * 2**20
        ),
    )
    results = call(images, cotangent, weights.reshape(TAPS, chan, chan), biases)
    outs, grads, kernels = pl.pallas_call(
        write_kernel,
        out_shape=(
            jax.ShapeDtypeStruct(images.shape, BF),
            jax.ShapeDtypeStruct(images.shape, BF),
            jax.ShapeDtypeStruct((TAPS, chan, chan), F32),
        ),
        in_specs=[inside] * 3,
        out_specs=(anywhere,) * 3,
        scratch_shapes=[vm((TAPS, chan, chan), F32), pltpu.SemaphoreType.DMA((3,))],
        compiler_params=pltpu.CompilerParams(vmem_limit_bytes=4 * 2**20),
    )(*results)
    return outs[None], grads[None], kernels.reshape(1, 3, 3, chan, chan)


def solution(mesh):
    placed = (
        P(None, "row", "col", None),
        P(None, "row", "col", None),
        P("segment", None, None, None, None),
        P("segment", None),
    )
    return jax.shard_map(
        body,
        mesh=mesh,
        in_specs=placed,
        out_specs=(
            P("segment", None, "row", "col", None),
            P("segment", None, "row", "col", None),
            P("segment", None, None, None, None),
        ),
        check_vma=False,
    )
```

```python
import functools
import math

import jax
import jax.numpy as jnp
from jax import lax
from jax.experimental import pallas as pl
from jax.experimental.pallas import tpu as pltpu
from jax.sharding import PartitionSpec as P

MESH = pl.DeviceIdType.MESH
BF = jnp.bfloat16
F32 = jnp.float32
SEG, MB, TAPS = 4, 2, 9
REACH = 6
GREACH = 4
WORDS = 5
CHUNK = 10
SIDE = 16
PAD = 8
DIRS = ((0, 1), (0, -1), (1, 0), (-1, 0), (1, 1), (1, -1), (-1, 1), (-1, -1))


def wrap(v, n):
    return jnp.where(v >= n, v - n, v)


def body_kernel(
    dims, images, cot, w, b, ox, og, full,
    xin, gin, wall, ball, aa, xs, gg, gs, gm, wf, wb,
    dw, s_core, r_core, d_half, r_main, r_tap_col, s_tap, r_tap_row,
    ss, rs, ls, words,
):
    rows, width, chan, nrow, ncol, scale = dims
    nz = nrow // 2
    hi = REACH + rows
    tall = rows + 2 * REACH
    wp = width + 2 * PAD
    half, strip = chan // 2, chan // 2 // ncol
    seg, row, col = lax.axis_index("segment"), lax.axis_index("row"), lax.axis_index("col")
    core, z = lax.rem(row, 2), lax.div(row, 2)
    sib = row + 1 - 2 * core

    def both(step):
        lax.fori_loop(0, MB, lambda m, carry: (step(m), carry)[1], 0)

    counter = [0]

    def fresh():
        counter[0] += 1
        return counter[0] - 1

    def remote(src, dst, dev, i, j=None):
        return pltpu.make_async_remote_copy(
            src_ref=src, dst_ref=dst, send_sem=ss.at[i], recv_sem=rs.at[i if j is None else j],
            device_id=dev, device_id_type=MESH,
        )

    mine = [
        pltpu.make_async_copy(images.at[m], xin.at[m, pl.ds(REACH, rows), pl.ds(SIDE, width)], ls.at[m])
        for m in range(MB)
    ]
    mine_g = pltpu.make_async_copy(cot, gin.at[:, pl.ds(GREACH, rows), pl.ds(SIDE, width)], ls.at[2])
    mine_w = pltpu.make_async_copy(w, wall.at[seg], ls.at[3])
    mine_b = pltpu.make_async_copy(b, ball.at[seg], ls.at[4])
    for copy in (*mine, mine_g, mine_w, mine_b):
        copy.start()

    barrier = pltpu.get_barrier_semaphore()

    def greet(s, r, c):
        pl.semaphore_signal(barrier, inc=1, device_id=(s, r, c), device_id_type=MESH)

    def inside(dr, dc):
        ok = jnp.bool_(True)
        if dr:
            ok = ok & (row + dr >= 0) & (row + dr < nrow)
        if dc:
            ok = ok & (col + dc >= 0) & (col + dc < ncol)
        return ok

    for k in range(1, SEG):
        greet(lax.rem(seg + k, SEG), row, col)
    beside_z = [lax.rem(row + 2, nrow), lax.rem(row + nrow - 2, nrow)]
    beside_y = [lax.rem(col + 1, ncol), lax.rem(col + ncol - 1, ncol)]
    for r in beside_z:
        greet(seg, r, col)
    for c in beside_y:
        greet(seg, row, c)
    met = SEG - 1 + 4
    for dr, dc in DIRS:
        if dr:
            pl.when(inside(dr, dc))(functools.partial(greet, seg, row + dr, col + dc))
            met = met + inside(dr, dc).astype(jnp.int32)
    pl.semaphore_wait(barrier, met)

    def pass_word(n):
        if n:
            pl.semaphore_wait(words.at[n - 1], 2)
        if n < nz // 2 - 1:
            for r in beside_z:
                pl.semaphore_signal(words.at[n], inc=1, device_id=(seg, r, col), device_id_type=MESH)
        elif n < WORDS:
            for c in beside_y:
                pl.semaphore_signal(words.at[n], inc=1, device_id=(seg, row, c), device_id_type=MESH)

    pass_word(0)

    def edges(source, target, reach):
        copies = []
        src_r = {1: (rows - reach, reach), -1: (0, reach), 0: (0, rows)}
        dst_r = {1: (0, reach), -1: (reach + rows, reach), 0: (reach, rows)}
        src_c = {1: (width - SIDE, SIDE), -1: (0, SIDE), 0: (0, width)}
        dst_c = {1: (0, SIDE), -1: (SIDE + width, SIDE), 0: (SIDE, width)}
        for dr, dc in DIRS:
            copies.append((
                remote(
                    source(pl.ds(*src_r[dr]), pl.ds(*src_c[dc])),
                    target(pl.ds(*dst_r[dr]), pl.ds(*dst_c[dc])),
                    (seg, row + dr, col + dc), fresh(),
                ),
                inside(dr, dc), inside(-dr, -dc),
            ))
        return copies

    def start_edges(copies):
        for copy, to, _ in copies:
            pl.when(to)(copy.start)

    def wait_edges(copies):
        for copy, _, of in copies:
            pl.when(of)(copy.wait_recv)

    x_edges = [
        edges(lambda r, c, m=m: images.at[m, r, c], lambda r, c, m=m: xin.at[m, r, c], REACH)
        for m in range(MB)
    ]
    g_edges = edges(lambda r, c: cot.at[:, r, c], lambda r, c: gin.at[:, r, c], GREACH)

    nxt, prv, far = lax.rem(seg + 1, SEG), lax.rem(seg + SEG - 1, SEG), lax.rem(seg + 2, SEG)
    own_rows = pl.ds(pl.multiple_of(half * core, half), half)
    first_q = pl.ds(pl.multiple_of(half * core, half), half // 2)
    second_q = pl.ds(pl.multiple_of(half * core + half // 2, half // 2), half // 2)
    sib_rows = pl.ds(pl.multiple_of(half * (1 - core), half), half)
    up, down = (nxt, row, col), (prv, row, col)
    beside = (seg, sib, col)
    i_ups, i_downs = (fresh(), fresh()), (fresh(), fresh())

    def outward(part, dev, i):
        return remote(w.at[:, part], wall.at[seg, :, part], dev, i)

    def onward(which, part, dev, i):
        return remote(wall.at[which, :, part], wall.at[which, :, part], dev, i)

    w_out = [
        outward(first_q, up, i_ups[0]), outward(second_q, down, i_downs[0]),
        outward(second_q, up, i_ups[1]), outward(first_q, down, i_downs[1]),
    ]
    got_prv = [onward(prv, first_q, up, i_ups[0]), onward(prv, second_q, up, i_ups[1])]
    got_nxt = [onward(nxt, second_q, down, i_downs[0]), onward(nxt, first_q, down, i_downs[1])]
    i_rup, i_rdown, i_s1, i_s2, i_s3 = fresh(), fresh(), fresh(), fresh(), fresh()
    relay_up, relay_down = onward(prv, first_q, up, i_rup), onward(nxt, second_q, down, i_rdown)
    got_rup, got_rdown = onward(far, first_q, up, i_rup), onward(far, second_q, down, i_rdown)
    share_prv, share_nxt = onward(prv, own_rows, beside, i_s1), onward(nxt, own_rows, beside, i_s2)
    share_far = onward(far, own_rows, beside, i_s3)
    got_s1, got_s2 = onward(prv, sib_rows, beside, i_s1), onward(nxt, sib_rows, beside, i_s2)
    got_s3 = onward(far, sib_rows, beside, i_s3)
    b_out, b_in = [], []
    for k in range(1, SEG):
        i = fresh()
        b_out.append(remote(b, ball.at[seg], (lax.rem(seg + k, SEG), row, col), i))
        b_in.append(remote(b, ball.at[lax.rem(seg + SEG - k, SEG)], (lax.rem(seg + k, SEG), row, col), i))

    start_edges(x_edges[0])
    for copy in w_out:
        copy.start()
    start_edges(x_edges[1])
    for copy in b_out:
        copy.start()
    start_edges(g_edges)

    def pass_near():
        got_prv[0].wait_recv()
        relay_up.start()
        got_nxt[0].wait_recv()
        relay_down.start()
        got_prv[1].wait_recv()
        share_prv.start()
        got_nxt[1].wait_recv()
        share_nxt.start()

    def pass_far():
        got_rup.wait_recv()
        got_rdown.wait_recv()
        share_far.start()

    def need(k):
        pl.when(seg == k)(mine_w.wait)
        pl.when(nxt == k)(got_s2.wait_recv)
        pl.when(far == k)(got_s3.wait_recv)
        pl.when(prv == k)(got_s1.wait_recv)

    def in_image(first, step, count):
        shape = (count, wp, chan)
        r = row * rows - REACH + first + step * lax.broadcasted_iota(jnp.int32, shape, 0)
        c = col * width - PAD + lax.broadcasted_iota(jnp.int32, shape, 1)
        return (r >= 0) & (r < nrow * rows) & (c >= 0) & (c < ncol * width)

    def trio(value):
        flat = value.reshape(-1, chan)
        n = flat.shape[0]
        return [
            v.astype(BF).reshape(value.shape)
            for v in (pltpu.roll(flat, 1, 0), flat, pltpu.roll(flat, n - 1, 0))
        ]

    def take_in(m):
        v = xin[m].astype(F32)[:, PAD : PAD + wp]
        v = jnp.where(in_image(0, 1, tall), v, 0.0)
        xs[m] = v.astype(BF).reshape(tall // 2, 2, wp, chan)
        for t, part in enumerate(trio(jnp.maximum(v, 0.0))):
            aa[0, m, :, :, :, pl.ds(t * chan, chan)] = part.reshape(tall // 2, 2, wp, chan)

    def wait_in(m):
        mine[m].wait()
        wait_edges(x_edges[m])

    def build(k):
        zero = jnp.zeros((3 * chan, chan), BF)
        for a in range(4):
            for h in range(2):
                ok = 0 <= a - h <= 2
                block = wall[k, 3 * (a - h) : 3 * (a - h) + 3].reshape(3 * chan, chan) if ok else zero
                wf[k, pl.ds(a * 3 * chan, 3 * chan), pl.ds(h * chan, chan)] = block
                for t in range(3):
                    p = h + 2 - a
                    tile = wall[k, 3 * p + 2 - t] if 0 <= p <= 2 else zero[:chan]
                    wb[k, pl.ds(h * chan, chan), pl.ds((3 * a + t) * chan, chan)] = tile

    def windows(ref, start, count):
        parts = []
        for a in range(4):
            r = start - 1 + a
            parts.append(ref[r // 2 : r // 2 + count // 2, r % 2].reshape(-1, 3 * chan))
        return jnp.concatenate(parts, axis=1)

    def chunked(multiply, finish, start, count, which):
        before = None
        for m in which:
            for c in range(0, count, CHUNK):
                now = (m, start + c, min(CHUNK, count - c))
                product = multiply(*now)
                if before:
                    finish(*before)
                before = (*now, product)
        finish(*before)

    def forward(s, which=range(MB)):
        start, count = (s + 1, tall - 2 * (s + 1)) if s < SEG - 1 else (REACH, rows)

        def multiply(m, first, n):
            return jnp.dot(windows(aa.at[s, m], first, n), wf[s], preferred_element_type=F32)

        def finish(m, first, n, y):
            n = n // 2
            for h in range(2):
                i, par = (first + h) // 2, (first + h) % 2
                x = xs[m, i : i + n, par].astype(F32)
                x = x + (y[:, h * chan : (h + 1) * chan].reshape(n, wp, chan) + ball[s][None])
                x = jnp.where(in_image(first + h, 2, n), x, 0.0).astype(BF)
                xs[m, i : i + n, par] = x
                if s < SEG - 1:
                    for t, part in enumerate(trio(jnp.maximum(x.astype(F32), 0.0))):
                        aa[s + 1, m, i : i + n, par, :, pl.ds(t * chan, chan)] = part

        chunked(multiply, finish, start, count, which)

    def block_of(ref, m):
        lo, up_to = REACH // 2, hi // 2
        return ref[m, lo:up_to].reshape(rows, wp, chan).astype(F32)

    def emit_x():
        def one(m):
            ox[m] = block_of(xs, m)[:, PAD : PAD + width].astype(BF)

        both(one)

    def emit_g():
        def one(m):
            og[m] = block_of(gs, m)[:, PAD : PAD + width].astype(BF)

        both(one)

    wait_in(0)
    take_in(0)
    pass_near()
    pass_word(1)
    pl.when(seg == 2)(pass_far)
    need(0)
    mine_b.wait()
    for copy in b_in:
        copy.wait_recv()
    build(0)
    forward(0, (0,))
    wait_in(1)
    take_in(1)
    forward(0, (1,))
    pass_word(2)
    pl.when(seg == 3)(pass_far)
    pl.when(seg == 0)(emit_x)
    need(1)
    build(1)
    forward(1)
    pass_word(3)
    pl.when(seg < 2)(pass_far)
    pl.when(seg == 1)(emit_x)
    need(2)
    build(2)
    forward(2)
    pass_word(4)
    pl.when(seg == 2)(emit_x)
    need(3)
    build(3)

    mine_g.wait()
    wait_edges(g_edges)
    edge = REACH - GREACH
    def take_in_grad(m):
        v = gin[m].astype(F32)[:, PAD : PAD + wp]
        v = jnp.where(in_image(edge, 1, tall - 2 * edge), v, 0.0)
        lo, n = edge // 2, tall // 2 - edge
        gs[m, lo : lo + n] = v.astype(BF).reshape(n, 2, wp, chan)
        for t, part in enumerate(trio(v)):
            gg[1, m, lo : lo + n, :, :, pl.ds(t * chan, chan)] = part.reshape(n, 2, wp, chan)
        nothing = jnp.zeros((2, wp, chan), BF)
        gm[m, 0:2] = nothing
        gm[m, rows + 2 : rows + 4] = nothing

    both(take_in_grad)

    def keep():
        c = lax.broadcasted_iota(jnp.int32, (rows, wp, chan), 1)
        def one(m):
            v = jnp.where((c >= PAD) & (c < PAD + width), block_of(gs, m), 0.0)
            gm[m, 2 : rows + 2] = v.astype(BF)

        both(one)

    def backward(k, which, slot, start, count, more):
        def multiply(m, first, n):
            return lax.dot_general(
                windows(gg.at[slot, m], first, n), wb[k], (((1,), (1,)), ((), ())),
                preferred_element_type=F32,
            )

        def finish(m, first, n, y):
            n = n // 2
            for h in range(2):
                i, par = (first + h) // 2, (first + h) % 2
                on = aa[k, m, i : i + n, par, :, pl.ds(chan, chan)].astype(F32) > 0.0
                g = gs[m, i : i + n, par].astype(F32)
                y_h = y[:, h * chan : (h + 1) * chan].reshape(n, wp, chan)
                g = (g + jnp.where(on, y_h, 0.0)).astype(BF)
                gs[m, i : i + n, par] = g
                if more:
                    for t, part in enumerate(trio(g.astype(F32))):
                        gg[1 - slot, m, i : i + n, par, :, pl.ds(t * chan, chan)] = part

        chunked(multiply, finish, start, count, which)

    for k in range(SEG - 1, 0, -1):

        def stage(k=k):
            backward(k, range(MB), k % 2, REACH - k, rows + 2 * k, True)

        pl.when(seg < k)(stage)
        if k == SEG - 1:
            pass_word(5)
    keep()

    def own_grad(m):
        backward(seg, (m,), lax.rem(seg, 2), REACH, rows, False)

    def last_x():
        forward(SEG - 1)
        emit_x()

    total = None
    for m in range(MB):
        lo, up_to = REACH // 2 - 1, hi // 2 + 1
        act = aa[seg, m, lo:up_to].reshape(rows + 4, wp, 3 * chan)[1 : rows + 3].reshape(-1, 3 * chan)
        grads = jnp.concatenate(
            [gm[m, 1 - p : rows + 3 - p].reshape(-1, chan) for p in (-1, 0, 1)], axis=1
        )
        term = lax.dot_general(act, grads, (((0,), (0,)), ((), ())), preferred_element_type=F32)
        total = term if total is None else total + term
    for p in range(3):
        for q in range(3):
            dw[3 * p + q] = total[q * chan : (q + 1) * chan, p * chan : (p + 1) * chan]

    def exchange(pairs):
        for copy, _ in pairs:
            copy.start()
        return pairs

    def arrived(pairs):
        for _, copy in pairs:
            copy.wait_recv()

    s_core[...] = dw[:, sib_rows].astype(BF)
    i = fresh()
    core_sum = remote(s_core, r_core, beside, i)
    core_sum.start()
    own_grad(0)
    core_sum.wait_recv()
    d_half[...] = (dw[:, own_rows] + r_core[...].astype(F32)).astype(BF)

    share = (TAPS - 1) // nz
    main = TAPS - 1
    last_tap = pl.ds(main, 1)
    cols = [wrap(col + k, ncol) for k in range(ncol)]
    zs = [wrap(z + k, nz) for k in range(nz)]
    strips = [pl.ds(pl.multiple_of(strip * c, strip), strip) for c in cols]
    places = [pl.ds(pl.multiple_of(half * core + strip * c, strip), strip) for c in cols]
    taps = [pl.ds(r * share, share) for r in zs]
    slots = [[c * nz + r for r in zs] for c in cols]
    steps = [(ky, kz) for ky in range(ncol) for kz in range(nz) if ky or kz]
    steps.sort(key=lambda s: -min(s[0], ncol - s[0]) - min(s[1], nz - s[1]))

    def device(ky, kz):
        return seg, 2 * zs[kz] + core, cols[ky]

    tap_col = [
        remote(d_half.at[last_tap, strips[k]], r_tap_col.at[k - 1], device(k, 0), fresh())
        for k in range(1, ncol)
    ]
    for copy in tap_col:
        copy.start()

    sums = []
    for ky, kz in steps:
        i = fresh()
        src = d_half.at[taps[kz], strips[ky]]
        sums.append((
            remote(src, r_main.at[slots[0][0]], device(ky, kz), i),
            remote(src, r_main.at[slots[-ky % ncol][-kz % nz]], device(ky, kz), i),
        ))
    for copy, _ in sums:
        copy.start()
    r_main[slots[0][0]] = d_half[taps[0], strips[0]]
    own_grad(1)
    emit_g()
    pl.when(seg == SEG - 1)(last_x)

    def total_of(ref, count):
        done = ref[0].astype(F32)
        for k in range(1, count):
            done = done + ref[k].astype(F32)
        return done

    for copy in tap_col:
        copy.wait_recv()
    tap = d_half[last_tap, strips[0]].astype(F32) + total_of(r_tap_col, ncol - 1)
    s_tap[...] = tap.astype(BF)
    r_tap_row[z] = tap.astype(BF)
    tap_row = []
    for k in range(1, nz):
        i = fresh()
        tap_row.append((
            remote(s_tap, r_tap_row.at[z], device(0, k), i),
            remote(s_tap, r_tap_row.at[zs[nz - k]], device(0, k), i),
        ))
    for copy, _ in tap_row:
        copy.start()

    spread = []
    for ky, kz in steps:
        i = fresh()
        src = full.at[taps[0], places[0]]
        spread.append((
            remote(src, src, device(ky, kz), i),
            remote(src, full.at[taps[-kz % nz], places[-ky % ncol]], device(ky, kz), i),
        ))
    for _, copy in sums:
        copy.wait_recv()
    full[taps[0], places[0]] = (total_of(r_main, ncol * nz) * scale).astype(BF)
    for copy, _ in spread:
        copy.start()
    for _, copy in tap_row:
        copy.wait_recv()
    full[last_tap, places[0]] = (total_of(r_tap_row, nz) * scale).astype(BF)
    tap_all = []
    for k in range(1, ncol):
        i = fresh()
        src = full.at[last_tap, places[0]]
        tap_all.append((
            remote(src, src, device(k, 0), i),
            remote(src, full.at[last_tap, places[ncol - k]], device(k, 0), i),
        ))
    for copy, _ in tap_all:
        copy.start()

    for copies in (*x_edges, g_edges):
        for copy, to, _ in copies:
            pl.when(to)(copy.wait_send)
    for copy in (*w_out, relay_up, relay_down, share_prv, share_nxt, share_far, *b_out):
        copy.wait_send()
    for copy, _ in (*sums, *tap_row):
        copy.wait_send()
    for copy in (core_sum, *tap_col):
        copy.wait_send()

    for _, copy in (*spread, *tap_all):
        copy.wait_recv()
    i = fresh()
    core_all = remote(full.at[:, own_rows], full.at[:, own_rows], beside, i)
    core_got = remote(full.at[:, own_rows], full.at[:, sib_rows], beside, i)
    core_all.start()
    for copy, _ in (*spread, *tap_all):
        copy.wait_send()
    core_got.wait_recv()
    core_all.wait_send()


def write_kernel(x, g, k, ox, og, ow, buf, sems):
    copies = [pltpu.make_async_copy(x, ox, sems.at[0]), pltpu.make_async_copy(g, og, sems.at[1])]
    for copy in copies:
        copy.start()
    buf[...] = k[...].astype(F32)
    copies.append(pltpu.make_async_copy(buf, ow, sems.at[2]))
    copies[-1].start()
    for copy in copies:
        copy.wait()


def body(images, cotangent, weights, biases):
    _, rows, width, chan = images.shape
    nrow, ncol = lax.axis_size("row"), lax.axis_size("col")
    nz = nrow // 2
    scale = 1.0 / math.sqrt(MB * rows * nrow * width * ncol)
    dims = (rows, width, chan, nrow, ncol, scale)
    tall, wp = rows + 2 * REACH, width + 2 * PAD
    wide = width + 2 * SIDE
    half, strip = chan // 2, chan // 2 // ncol
    share = (TAPS - 1) // nz
    vm = pltpu.VMEM
    chips = ncol * nz
    sems = 8 * 3 + 9 + 3 + 2 + 2 * (chips - 1) + 2 * (ncol - 1) + nz - 1
    anywhere = pl.BlockSpec(memory_space=pl.ANY)
    inside = pl.BlockSpec(memory_space=pltpu.VMEM)
    call = pl.pallas_call(
        functools.partial(body_kernel, dims),
        out_shape=(vm(images.shape, BF), vm(images.shape, BF), vm((TAPS, chan, chan), BF)),
        in_specs=[anywhere] * 4,
        out_specs=(inside,) * 3,
        scratch_shapes=[
            vm((MB, tall, wide, chan), BF),
            vm((MB, rows + 2 * GREACH, wide, chan), BF),
            vm((SEG, TAPS, chan, chan), BF),
            vm((SEG, 1, chan), F32),
            vm((SEG, MB, tall // 2, 2, wp, 3 * chan), BF),
            vm((MB, tall // 2, 2, wp, chan), BF),
            vm((2, MB, tall // 2, 2, wp, 3 * chan), BF),
            vm((MB, tall // 2, 2, wp, chan), BF),
            vm((MB, rows + 4, wp, chan), BF),
            vm((SEG, 12 * chan, 2 * chan), BF),
            vm((SEG, 2 * chan, 12 * chan), BF),
            vm((TAPS, chan, chan), F32),
            vm((TAPS, half, chan), BF),
            vm((TAPS, half, chan), BF),
            vm((TAPS, half, chan), BF),
            vm((chips, share, strip, chan), BF),
            vm((ncol - 1, 1, strip, chan), BF),
            vm((1, strip, chan), BF),
            vm((nz, 1, strip, chan), BF),
            pltpu.SemaphoreType.DMA((sems,)),
            pltpu.SemaphoreType.DMA((sems,)),
            pltpu.SemaphoreType.DMA((5,)),
            pltpu.SemaphoreType.REGULAR((WORDS,)),
        ],
        compiler_params=pltpu.CompilerParams(
            collective_id=0, has_side_effects=True, vmem_limit_bytes=56 * 2**20
        ),
    )
    results = call(images, cotangent, weights.reshape(TAPS, chan, chan), biases)
    outs, grads, kernels = pl.pallas_call(
        write_kernel,
        out_shape=(
            jax.ShapeDtypeStruct(images.shape, BF),
            jax.ShapeDtypeStruct(images.shape, BF),
            jax.ShapeDtypeStruct((TAPS, chan, chan), F32),
        ),
        in_specs=[inside] * 3,
        out_specs=(anywhere,) * 3,
        scratch_shapes=[vm((TAPS, chan, chan), F32), pltpu.SemaphoreType.DMA((3,))],
        compiler_params=pltpu.CompilerParams(vmem_limit_bytes=4 * 2**20),
    )(*results)
    return outs[None], grads[None], kernels.reshape(1, 3, 3, chan, chan)


def solution(mesh):
    placed = (
        P(None, "row", "col", None),
        P(None, "row", "col", None),
        P("segment", None, None, None, None),
        P("segment", None),
    )
    return jax.shard_map(
        body,
        mesh=mesh,
        in_specs=placed,
        out_specs=(
            P("segment", None, "row", "col", None),
            P("segment", None, "row", "col", None),
            P("segment", None, None, None, None),
        ),
        check_vma=False,
    )
```

```python
import functools
import math

import jax
import jax.numpy as jnp
from jax import lax
from jax.experimental import pallas as pl
from jax.experimental.pallas import tpu as pltpu
from jax.sharding import PartitionSpec as P

MESH = pl.DeviceIdType.MESH
BF = jnp.bfloat16
F32 = jnp.float32
SEG, MB, TAPS = 4, 2, 9
REACH = 6
GREACH = 4
WORDS = 5
CHUNK = 10
SIDE = 16
PAD = 8
DIRS = ((0, 1), (0, -1), (1, 0), (-1, 0), (1, 1), (1, -1), (-1, 1), (-1, -1))


def wrap(v, n):
    return jnp.where(v >= n, v - n, v)


def body_kernel(
    dims, images, cot, w, b, ox, og, full,
    xin, gin, wall, ball, aa, xs, gg, gs, gm, mask,
    dw, s_core, r_core, d_half, r_main, r_tap_col, s_tap, r_tap_row,
    ss, rs, ls, words,
):
    rows, width, chan, nrow, ncol, scale = dims
    nz = nrow // 2
    hi = REACH + rows
    tall = rows + 2 * REACH
    wp = width + 2 * PAD
    half, strip = chan // 2, chan // 2 // ncol
    seg, row, col = lax.axis_index("segment"), lax.axis_index("row"), lax.axis_index("col")
    core, z = lax.rem(row, 2), lax.div(row, 2)
    sib = row + 1 - 2 * core

    def both(step):
        lax.fori_loop(0, MB, lambda m, carry: (step(m), carry)[1], 0)

    counter = [0]

    def fresh():
        counter[0] += 1
        return counter[0] - 1

    def remote(src, dst, dev, i, j=None):
        return pltpu.make_async_remote_copy(
            src_ref=src, dst_ref=dst, send_sem=ss.at[i], recv_sem=rs.at[i if j is None else j],
            device_id=dev, device_id_type=MESH,
        )

    mine = [
        pltpu.make_async_copy(images.at[m], xin.at[m, pl.ds(REACH, rows), pl.ds(SIDE, width)], ls.at[m])
        for m in range(MB)
    ]
    mine_g = pltpu.make_async_copy(cot, gin.at[:, pl.ds(GREACH, rows), pl.ds(SIDE, width)], ls.at[2])
    mine_w = pltpu.make_async_copy(w, wall.at[seg], ls.at[3])
    mine_b = pltpu.make_async_copy(b, ball.at[seg], ls.at[4])
    for copy in (*mine, mine_g, mine_w, mine_b):
        copy.start()

    barrier = pltpu.get_barrier_semaphore()

    def greet(s, r, c):
        pl.semaphore_signal(barrier, inc=1, device_id=(s, r, c), device_id_type=MESH)

    def inside(dr, dc):
        ok = jnp.bool_(True)
        if dr:
            ok = ok & (row + dr >= 0) & (row + dr < nrow)
        if dc:
            ok = ok & (col + dc >= 0) & (col + dc < ncol)
        return ok

    for k in range(1, SEG):
        greet(lax.rem(seg + k, SEG), row, col)
    beside_z = [lax.rem(row + 2, nrow), lax.rem(row + nrow - 2, nrow)]
    beside_y = [lax.rem(col + 1, ncol), lax.rem(col + ncol - 1, ncol)]
    for r in beside_z:
        greet(seg, r, col)
    for c in beside_y:
        greet(seg, row, c)
    met = SEG - 1 + 4
    for dr, dc in DIRS:
        if dr:
            pl.when(inside(dr, dc))(functools.partial(greet, seg, row + dr, col + dc))
            met = met + inside(dr, dc).astype(jnp.int32)
    pl.semaphore_wait(barrier, met)

    def pass_word(n):
        if n:
            pl.semaphore_wait(words.at[n - 1], 2)
        if n < nz // 2 - 1:
            for r in beside_z:
                pl.semaphore_signal(words.at[n], inc=1, device_id=(seg, r, col), device_id_type=MESH)
        elif n < WORDS:
            for c in beside_y:
                pl.semaphore_signal(words.at[n], inc=1, device_id=(seg, row, c), device_id_type=MESH)

    pass_word(0)

    def edges(source, target, reach):
        copies = []
        src_r = {1: (rows - reach, reach), -1: (0, reach), 0: (0, rows)}
        dst_r = {1: (0, reach), -1: (reach + rows, reach), 0: (reach, rows)}
        src_c = {1: (width - SIDE, SIDE), -1: (0, SIDE), 0: (0, width)}
        dst_c = {1: (0, SIDE), -1: (SIDE + width, SIDE), 0: (SIDE, width)}
        for dr, dc in DIRS:
            copies.append((
                remote(
                    source(pl.ds(*src_r[dr]), pl.ds(*src_c[dc])),
                    target(pl.ds(*dst_r[dr]), pl.ds(*dst_c[dc])),
                    (seg, row + dr, col + dc), fresh(),
                ),
                inside(dr, dc), inside(-dr, -dc),
            ))
        return copies

    def start_edges(copies):
        for copy, to, _ in copies:
            pl.when(to)(copy.start)

    def wait_edges(copies):
        for copy, _, of in copies:
            pl.when(of)(copy.wait_recv)

    x_edges = [
        edges(lambda r, c, m=m: images.at[m, r, c], lambda r, c, m=m: xin.at[m, r, c], REACH)
        for m in range(MB)
    ]
    g_edges = edges(lambda r, c: cot.at[:, r, c], lambda r, c: gin.at[:, r, c], GREACH)

    nxt, prv, far = lax.rem(seg + 1, SEG), lax.rem(seg + SEG - 1, SEG), lax.rem(seg + 2, SEG)
    own_rows = pl.ds(pl.multiple_of(half * core, half), half)
    first_q = pl.ds(pl.multiple_of(half * core, half), half // 2)
    second_q = pl.ds(pl.multiple_of(half * core + half // 2, half // 2), half // 2)
    sib_rows = pl.ds(pl.multiple_of(half * (1 - core), half), half)
    up, down = (nxt, row, col), (prv, row, col)
    beside = (seg, sib, col)
    i_ups, i_downs = (fresh(), fresh()), (fresh(), fresh())

    def outward(part, dev, i):
        return remote(w.at[:, part], wall.at[seg, :, part], dev, i)

    def onward(which, part, dev, i):
        return remote(wall.at[which, :, part], wall.at[which, :, part], dev, i)

    w_out = [
        outward(first_q, up, i_ups[0]), outward(second_q, down, i_downs[0]),
        outward(second_q, up, i_ups[1]), outward(first_q, down, i_downs[1]),
    ]
    got_prv = [onward(prv, first_q, up, i_ups[0]), onward(prv, second_q, up, i_ups[1])]
    got_nxt = [onward(nxt, second_q, down, i_downs[0]), onward(nxt, first_q, down, i_downs[1])]
    i_rup, i_rdown, i_s1, i_s2, i_s3 = fresh(), fresh(), fresh(), fresh(), fresh()
    relay_up, relay_down = onward(prv, first_q, up, i_rup), onward(nxt, second_q, down, i_rdown)
    got_rup, got_rdown = onward(far, first_q, up, i_rup), onward(far, second_q, down, i_rdown)
    share_prv, share_nxt = onward(prv, own_rows, beside, i_s1), onward(nxt, own_rows, beside, i_s2)
    share_far = onward(far, own_rows, beside, i_s3)
    got_s1, got_s2 = onward(prv, sib_rows, beside, i_s1), onward(nxt, sib_rows, beside, i_s2)
    got_s3 = onward(far, sib_rows, beside, i_s3)
    b_out, b_in = [], []
    for k in range(1, SEG):
        i = fresh()
        b_out.append(remote(b, ball.at[seg], (lax.rem(seg + k, SEG), row, col), i))
        b_in.append(remote(b, ball.at[lax.rem(seg + SEG - k, SEG)], (lax.rem(seg + k, SEG), row, col), i))

    for copy in w_out:
        copy.start()
    start_edges(x_edges[0])
    start_edges(x_edges[1])
    for copy in b_out:
        copy.start()
    start_edges(g_edges)

    def pass_near():
        got_prv[0].wait_recv()
        relay_up.start()
        got_nxt[0].wait_recv()
        relay_down.start()
        got_prv[1].wait_recv()
        share_prv.start()
        got_nxt[1].wait_recv()
        share_nxt.start()

    def pass_far():
        got_rup.wait_recv()
        got_rdown.wait_recv()
        share_far.start()

    def need(k):
        pl.when(seg == k)(mine_w.wait)
        pl.when(nxt == k)(got_s2.wait_recv)
        pl.when(far == k)(got_s3.wait_recv)
        pl.when(prv == k)(got_s1.wait_recv)

    def in_image(first, step, count):
        shape = (count, wp, chan)
        r = row * rows - REACH + first + step * lax.broadcasted_iota(jnp.int32, shape, 0)
        c = col * width - PAD + lax.broadcasted_iota(jnp.int32, shape, 1)
        return (r >= 0) & (r < nrow * rows) & (c >= 0) & (c < ncol * width)

    mask[...] = jnp.where(in_image(0, 1, tall), 1.0, 0.0).reshape(mask.shape)

    def trio(value):
        flat = value.reshape(-1, chan)
        n = flat.shape[0]
        return [
            v.astype(BF).reshape(value.shape)
            for v in (pltpu.roll(flat, 1, 0), flat, pltpu.roll(flat, n - 1, 0))
        ]

    def take_in(m):
        v = xin[m].astype(F32)[:, PAD : PAD + wp]
        v = jnp.where(mask[...].reshape(tall, wp, chan) > 0.0, v, 0.0)
        xs[m] = v.astype(BF).reshape(tall // 2, 2, wp, chan)
        for t, part in enumerate(trio(jnp.maximum(v, 0.0))):
            aa[0, m, :, :, :, pl.ds(t * chan, chan)] = part.reshape(tall // 2, 2, wp, chan)

    def wait_in(m):
        mine[m].wait()
        wait_edges(x_edges[m])

    zero = jnp.zeros((chan, chan), BF)

    def tile(k, p, q):
        return wall[k, 3 * p + q] if 0 <= p <= 2 else zero

    def there(k):
        rows_of = [
            jnp.concatenate([tile(k, a, t), tile(k, a - 1, t)], axis=1)
            for a in range(4) for t in range(3)
        ]
        return jnp.concatenate(rows_of, axis=0)

    def back(k):
        rows_of = [
            jnp.concatenate([tile(k, h + 2 - a, 2 - t) for a in range(4) for t in range(3)], axis=1)
            for h in range(2)
        ]
        return jnp.concatenate(rows_of, axis=0)

    def windows(ref, start, count):
        parts = []
        for a in range(4):
            r = start - 1 + a
            parts.append(ref[r // 2 : r // 2 + count // 2, r % 2].reshape(-1, 3 * chan))
        return jnp.concatenate(parts, axis=1)

    def chunked(multiply, finish, start, count, which):
        before = None
        for m in which:
            for c in range(0, count, CHUNK):
                now = (m, start + c, min(CHUNK, count - c))
                product = multiply(*now)
                if before:
                    finish(*before)
                before = (*now, product)
        finish(*before)

    def forward(s, which=range(MB)):
        start, count = (s + 1, tall - 2 * (s + 1)) if s < SEG - 1 else (REACH, rows)

        def multiply(m, first, n):
            return jnp.dot(windows(aa.at[s, m], first, n), there(s), preferred_element_type=F32)

        def finish(m, first, n, y):
            n = n // 2
            for h in range(2):
                i, par = (first + h) // 2, (first + h) % 2
                x = xs[m, i : i + n, par].astype(F32)
                x = x + (y[:, h * chan : (h + 1) * chan].reshape(n, wp, chan) + ball[s][None])
                x = jnp.where(mask[i : i + n, par] > 0.0, x, 0.0).astype(BF)
                xs[m, i : i + n, par] = x
                if s < SEG - 1:
                    for t, part in enumerate(trio(jnp.maximum(x.astype(F32), 0.0))):
                        aa[s + 1, m, i : i + n, par, :, pl.ds(t * chan, chan)] = part

        chunked(multiply, finish, start, count, which)

    def block_of(ref, m):
        lo, up_to = REACH // 2, hi // 2
        return ref[m, lo:up_to].reshape(rows, wp, chan).astype(F32)

    def emit_x():
        def one(m):
            ox[m] = block_of(xs, m)[:, PAD : PAD + width].astype(BF)

        both(one)

    def emit_g():
        def one(m):
            og[m] = block_of(gs, m)[:, PAD : PAD + width].astype(BF)

        both(one)

    wait_in(0)
    take_in(0)
    pass_near()
    pass_word(1)
    pl.when(seg == 2)(pass_far)
    need(0)
    mine_b.wait()
    for copy in b_in:
        copy.wait_recv()
    forward(0, (0,))
    wait_in(1)
    take_in(1)
    forward(0, (1,))
    pass_word(2)
    pl.when(seg == 3)(pass_far)
    pl.when(seg == 0)(emit_x)
    need(1)
    forward(1)
    pass_word(3)
    pl.when(seg < 2)(pass_far)
    pl.when(seg == 1)(emit_x)
    mine_g.wait()
    wait_edges(g_edges)
    edge = REACH - GREACH

    def take_in_grad(m):
        v = gin[m].astype(F32)[:, PAD : PAD + wp]
        lo, n = edge // 2, tall // 2 - edge
        v = jnp.where(mask[lo : lo + n].reshape(v.shape) > 0.0, v, 0.0)
        gs[m, lo : lo + n] = v.astype(BF).reshape(n, 2, wp, chan)
        for t, part in enumerate(trio(v)):
            gg[1, m, lo : lo + n, :, :, pl.ds(t * chan, chan)] = part.reshape(n, 2, wp, chan)
        nothing = jnp.zeros((2, wp, chan), BF)
        gm[m, 0:2] = nothing
        gm[m, rows + 2 : rows + 4] = nothing

    both(take_in_grad)
    need(2)
    forward(2)
    pass_word(4)
    pl.when(seg == 2)(emit_x)
    need(3)

    def keep():
        c = lax.broadcasted_iota(jnp.int32, (rows, wp, chan), 1)
        def one(m):
            v = jnp.where((c >= PAD) & (c < PAD + width), block_of(gs, m), 0.0)
            gm[m, 2 : rows + 2] = v.astype(BF)

        both(one)

    def backward(k, which, slot, start, count, more):
        def multiply(m, first, n):
            return lax.dot_general(
                windows(gg.at[slot, m], first, n), back(k), (((1,), (1,)), ((), ())),
                preferred_element_type=F32,
            )

        def finish(m, first, n, y):
            n = n // 2
            for h in range(2):
                i, par = (first + h) // 2, (first + h) % 2
                on = aa[k, m, i : i + n, par, :, pl.ds(chan, chan)].astype(F32) > 0.0
                g = gs[m, i : i + n, par].astype(F32)
                y_h = y[:, h * chan : (h + 1) * chan].reshape(n, wp, chan)
                g = (g + jnp.where(on, y_h, 0.0)).astype(BF)
                gs[m, i : i + n, par] = g
                if more:
                    for t, part in enumerate(trio(g.astype(F32))):
                        gg[1 - slot, m, i : i + n, par, :, pl.ds(t * chan, chan)] = part

        chunked(multiply, finish, start, count, which)

    for k in range(SEG - 1, 0, -1):

        def stage(k=k):
            backward(k, range(MB), k % 2, REACH - k, rows + 2 * k, True)

        pl.when(seg < k)(stage)
        if k == SEG - 1:
            pass_word(5)
    keep()

    def own_grad(m):
        backward(seg, (m,), lax.rem(seg, 2), REACH, rows, False)

    def last_x():
        forward(SEG - 1)
        emit_x()

    total = None
    for m in range(MB):
        lo, up_to = REACH // 2 - 1, hi // 2 + 1
        act = aa[seg, m, lo:up_to].reshape(rows + 4, wp, 3 * chan)[1 : rows + 3].reshape(-1, 3 * chan)
        grads = jnp.concatenate(
            [gm[m, 1 - p : rows + 3 - p].reshape(-1, chan) for p in (-1, 0, 1)], axis=1
        )
        term = lax.dot_general(act, grads, (((0,), (0,)), ((), ())), preferred_element_type=F32)
        total = term if total is None else total + term
    for p in range(3):
        for q in range(3):
            dw[3 * p + q] = total[q * chan : (q + 1) * chan, p * chan : (p + 1) * chan]

    def exchange(pairs):
        for copy, _ in pairs:
            copy.start()
        return pairs

    def arrived(pairs):
        for _, copy in pairs:
            copy.wait_recv()

    s_core[...] = dw[:, sib_rows].astype(BF)
    i = fresh()
    core_sum = remote(s_core, r_core, beside, i)
    core_sum.start()
    own_grad(0)
    core_sum.wait_recv()
    d_half[...] = (dw[:, own_rows] + r_core[...].astype(F32)).astype(BF)

    share = (TAPS - 1) // nz
    main = TAPS - 1
    last_tap = pl.ds(main, 1)
    cols = [wrap(col + k, ncol) for k in range(ncol)]
    zs = [wrap(z + k, nz) for k in range(nz)]
    strips = [pl.ds(pl.multiple_of(strip * c, strip), strip) for c in cols]
    places = [pl.ds(pl.multiple_of(half * core + strip * c, strip), strip) for c in cols]
    taps = [pl.ds(r * share, share) for r in zs]
    slots = [[c * nz + r for r in zs] for c in cols]
    steps = [(ky, kz) for ky in range(ncol) for kz in range(nz) if ky or kz]
    steps.sort(key=lambda s: -min(s[0], ncol - s[0]) - min(s[1], nz - s[1]))

    def device(ky, kz):
        return seg, 2 * zs[kz] + core, cols[ky]

    tap_col = [
        remote(d_half.at[last_tap, strips[k]], r_tap_col.at[k - 1], device(k, 0), fresh())
        for k in range(1, ncol)
    ]
    for copy in tap_col:
        copy.start()

    sums = []
    for ky, kz in steps:
        i = fresh()
        src = d_half.at[taps[kz], strips[ky]]
        sums.append((
            remote(src, r_main.at[slots[0][0]], device(ky, kz), i),
            remote(src, r_main.at[slots[-ky % ncol][-kz % nz]], device(ky, kz), i),
        ))
    for copy, _ in sums:
        copy.start()
    r_main[slots[0][0]] = d_half[taps[0], strips[0]]
    own_grad(1)
    emit_g()
    pl.when(seg == SEG - 1)(last_x)

    def total_of(ref, count):
        done = ref[0].astype(F32)
        for k in range(1, count):
            done = done + ref[k].astype(F32)
        return done

    for copy in tap_col:
        copy.wait_recv()
    tap = d_half[last_tap, strips[0]].astype(F32) + total_of(r_tap_col, ncol - 1)
    s_tap[...] = tap.astype(BF)
    r_tap_row[z] = tap.astype(BF)
    tap_row = []
    for k in range(1, nz):
        i = fresh()
        tap_row.append((
            remote(s_tap, r_tap_row.at[z], device(0, k), i),
            remote(s_tap, r_tap_row.at[zs[nz - k]], device(0, k), i),
        ))
    for copy, _ in tap_row:
        copy.start()

    spread = []
    for ky, kz in steps:
        i = fresh()
        src = full.at[taps[0], places[0]]
        spread.append((
            remote(src, src, device(ky, kz), i),
            remote(src, full.at[taps[-kz % nz], places[-ky % ncol]], device(ky, kz), i),
        ))
    for _, copy in sums:
        copy.wait_recv()
    full[taps[0], places[0]] = (total_of(r_main, ncol * nz) * scale).astype(BF)
    for copy, _ in spread:
        copy.start()
    for _, copy in tap_row:
        copy.wait_recv()
    full[last_tap, places[0]] = (total_of(r_tap_row, nz) * scale).astype(BF)
    tap_all = []
    for k in range(1, ncol):
        i = fresh()
        src = full.at[last_tap, places[0]]
        tap_all.append((
            remote(src, src, device(k, 0), i),
            remote(src, full.at[last_tap, places[ncol - k]], device(k, 0), i),
        ))
    for copy, _ in tap_all:
        copy.start()

    for copies in (*x_edges, g_edges):
        for copy, to, _ in copies:
            pl.when(to)(copy.wait_send)
    for copy in (*w_out, relay_up, relay_down, share_prv, share_nxt, share_far, *b_out):
        copy.wait_send()
    for copy, _ in (*sums, *tap_row):
        copy.wait_send()
    for copy in (core_sum, *tap_col):
        copy.wait_send()

    for _, copy in (*spread, *tap_all):
        copy.wait_recv()
    i = fresh()
    core_all = remote(full.at[:, own_rows], full.at[:, own_rows], beside, i)
    core_got = remote(full.at[:, own_rows], full.at[:, sib_rows], beside, i)
    core_all.start()
    for copy, _ in (*spread, *tap_all):
        copy.wait_send()
    core_got.wait_recv()
    core_all.wait_send()


def write_kernel(x, g, k, ox, og, ow, buf, sems):
    copies = [pltpu.make_async_copy(x, ox, sems.at[0]), pltpu.make_async_copy(g, og, sems.at[1])]
    for copy in copies:
        copy.start()
    buf[...] = k[...].astype(F32)
    copies.append(pltpu.make_async_copy(buf, ow, sems.at[2]))
    copies[-1].start()
    for copy in copies:
        copy.wait()


def body(images, cotangent, weights, biases):
    _, rows, width, chan = images.shape
    nrow, ncol = lax.axis_size("row"), lax.axis_size("col")
    nz = nrow // 2
    scale = 1.0 / math.sqrt(MB * rows * nrow * width * ncol)
    dims = (rows, width, chan, nrow, ncol, scale)
    tall, wp = rows + 2 * REACH, width + 2 * PAD
    wide = width + 2 * SIDE
    half, strip = chan // 2, chan // 2 // ncol
    share = (TAPS - 1) // nz
    vm = pltpu.VMEM
    chips = ncol * nz
    sems = 8 * 3 + 9 + 3 + 2 + 2 * (chips - 1) + 2 * (ncol - 1) + nz - 1
    anywhere = pl.BlockSpec(memory_space=pl.ANY)
    inside = pl.BlockSpec(memory_space=pltpu.VMEM)
    call = pl.pallas_call(
        functools.partial(body_kernel, dims),
        out_shape=(vm(images.shape, BF), vm(images.shape, BF), vm((TAPS, chan, chan), BF)),
        in_specs=[anywhere] * 4,
        out_specs=(inside,) * 3,
        scratch_shapes=[
            vm((MB, tall, wide, chan), BF),
            vm((MB, rows + 2 * GREACH, wide, chan), BF),
            vm((SEG, TAPS, chan, chan), BF),
            vm((SEG, 1, chan), F32),
            vm((SEG, MB, tall // 2, 2, wp, 3 * chan), BF),
            vm((MB, tall // 2, 2, wp, chan), BF),
            vm((2, MB, tall // 2, 2, wp, 3 * chan), BF),
            vm((MB, tall // 2, 2, wp, chan), BF),
            vm((MB, rows + 4, wp, chan), BF),
            vm((tall // 2, 2, wp, chan), F32),
            vm((TAPS, chan, chan), F32),
            vm((TAPS, half, chan), BF),
            vm((TAPS, half, chan), BF),
            vm((TAPS, half, chan), BF),
            vm((chips, share, strip, chan), BF),
            vm((ncol - 1, 1, strip, chan), BF),
            vm((1, strip, chan), BF),
            vm((nz, 1, strip, chan), BF),
            pltpu.SemaphoreType.DMA((sems,)),
            pltpu.SemaphoreType.DMA((sems,)),
            pltpu.SemaphoreType.DMA((5,)),
            pltpu.SemaphoreType.REGULAR((WORDS,)),
        ],
        compiler_params=pltpu.CompilerParams(
            collective_id=0, has_side_effects=True, vmem_limit_bytes=56 * 2**20
        ),
    )
    results = call(images, cotangent, weights.reshape(TAPS, chan, chan), biases)
    outs, grads, kernels = pl.pallas_call(
        write_kernel,
        out_shape=(
            jax.ShapeDtypeStruct(images.shape, BF),
            jax.ShapeDtypeStruct(images.shape, BF),
            jax.ShapeDtypeStruct((TAPS, chan, chan), F32),
        ),
        in_specs=[inside] * 3,
        out_specs=(anywhere,) * 3,
        scratch_shapes=[vm((TAPS, chan, chan), F32), pltpu.SemaphoreType.DMA((3,))],
        compiler_params=pltpu.CompilerParams(vmem_limit_bytes=4 * 2**20),
    )(*results)
    return outs[None], grads[None], kernels.reshape(1, 3, 3, chan, chan)


def solution(mesh):
    placed = (
        P(None, "row", "col", None),
        P(None, "row", "col", None),
        P("segment", None, None, None, None),
        P("segment", None),
    )
    return jax.shard_map(
        body,
        mesh=mesh,
        in_specs=placed,
        out_specs=(
            P("segment", None, "row", "col", None),
            P("segment", None, "row", "col", None),
            P("segment", None, None, None, None),
        ),
        check_vma=False,
    )
```

```python
import functools
import math

import jax
import jax.numpy as jnp
from jax import lax
from jax.experimental import pallas as pl
from jax.experimental.pallas import tpu as pltpu
from jax.sharding import PartitionSpec as P

MESH = pl.DeviceIdType.MESH
BF = jnp.bfloat16
F32 = jnp.float32
SEG, MB, TAPS = 4, 2, 9
REACH = 6
GREACH = 4
WORDS = 5
CHUNK = 10
SIDE = 16
PAD = 8
DIRS = ((1, 1), (1, -1), (-1, 1), (-1, -1), (1, 0), (-1, 0), (0, 1), (0, -1))


def wrap(v, n):
    return jnp.where(v >= n, v - n, v)


def body_kernel(
    dims, images, cot, w, b, ox, og, full,
    xin, gin, wall, ball, aa, xs, gg, gs, gm, mask,
    dw, s_core, r_core, d_half, r_main, r_tap_col, s_tap, r_tap_row,
    ss, rs, ls, words,
):
    rows, width, chan, nrow, ncol, scale = dims
    nz = nrow // 2
    hi = REACH + rows
    tall = rows + 2 * REACH
    wp = width + 2 * PAD
    half, strip = chan // 2, chan // 2 // ncol
    seg, row, col = lax.axis_index("segment"), lax.axis_index("row"), lax.axis_index("col")
    core, z = lax.rem(row, 2), lax.div(row, 2)
    sib = row + 1 - 2 * core

    def both(step):
        lax.fori_loop(0, MB, lambda m, carry: (step(m), carry)[1], 0)

    counter = [0]

    def fresh():
        counter[0] += 1
        return counter[0] - 1

    def remote(src, dst, dev, i, j=None):
        return pltpu.make_async_remote_copy(
            src_ref=src, dst_ref=dst, send_sem=ss.at[i], recv_sem=rs.at[i if j is None else j],
            device_id=dev, device_id_type=MESH,
        )

    barrier = pltpu.get_barrier_semaphore()

    def greet(s, r, c):
        pl.semaphore_signal(barrier, inc=1, device_id=(s, r, c), device_id_type=MESH)

    def inside(dr, dc):
        ok = jnp.bool_(True)
        if dr:
            ok = ok & (row + dr >= 0) & (row + dr < nrow)
        if dc:
            ok = ok & (col + dc >= 0) & (col + dc < ncol)
        return ok

    met = SEG - 1 + 4
    for dr, dc in DIRS:
        if dr:
            pl.when(inside(dr, dc))(functools.partial(greet, seg, row + dr, col + dc))
            met = met + inside(dr, dc).astype(jnp.int32)
    for k in range(1, SEG):
        greet(lax.rem(seg + k, SEG), row, col)
    beside_z = [lax.rem(row + 2, nrow), lax.rem(row + nrow - 2, nrow)]
    beside_y = [lax.rem(col + 1, ncol), lax.rem(col + ncol - 1, ncol)]
    for r in beside_z:
        greet(seg, r, col)
    for c in beside_y:
        greet(seg, row, c)

    mine = [
        pltpu.make_async_copy(images.at[m], xin.at[m, pl.ds(REACH, rows), pl.ds(SIDE, width)], ls.at[m])
        for m in range(MB)
    ]
    mine_g = pltpu.make_async_copy(cot, gin.at[:, pl.ds(GREACH, rows), pl.ds(SIDE, width)], ls.at[2])
    mine_w = pltpu.make_async_copy(w, wall.at[seg], ls.at[3])
    mine_b = pltpu.make_async_copy(b, ball.at[seg], ls.at[4])
    for copy in (*mine, mine_g, mine_w, mine_b):
        copy.start()

    pl.semaphore_wait(barrier, met)

    def pass_word(n):
        if n:
            pl.semaphore_wait(words.at[n - 1], 2)
        if n < nz // 2 - 1:
            for r in beside_z:
                pl.semaphore_signal(words.at[n], inc=1, device_id=(seg, r, col), device_id_type=MESH)
        elif n < WORDS:
            for c in beside_y:
                pl.semaphore_signal(words.at[n], inc=1, device_id=(seg, row, c), device_id_type=MESH)

    pass_word(0)

    def edges(source, target, reach):
        copies = []
        src_r = {1: (rows - reach, reach), -1: (0, reach), 0: (0, rows)}
        dst_r = {1: (0, reach), -1: (reach + rows, reach), 0: (reach, rows)}
        src_c = {1: (width - SIDE, SIDE), -1: (0, SIDE), 0: (0, width)}
        dst_c = {1: (0, SIDE), -1: (SIDE + width, SIDE), 0: (SIDE, width)}
        for dr, dc in DIRS:
            copies.append((
                remote(
                    source(pl.ds(*src_r[dr]), pl.ds(*src_c[dc])),
                    target(pl.ds(*dst_r[dr]), pl.ds(*dst_c[dc])),
                    (seg, row + dr, col + dc), fresh(),
                ),
                inside(dr, dc), inside(-dr, -dc),
            ))
        return copies

    def start_edges(copies):
        for copy, to, _ in copies:
            pl.when(to)(copy.start)

    def wait_edges(copies):
        for copy, _, of in reversed(copies):
            pl.when(of)(copy.wait_recv)

    x_edges = [
        edges(lambda r, c, m=m: images.at[m, r, c], lambda r, c, m=m: xin.at[m, r, c], REACH)
        for m in range(MB)
    ]
    g_edges = edges(lambda r, c: cot.at[:, r, c], lambda r, c: gin.at[:, r, c], GREACH)

    nxt, prv, far = lax.rem(seg + 1, SEG), lax.rem(seg + SEG - 1, SEG), lax.rem(seg + 2, SEG)
    own_rows = pl.ds(pl.multiple_of(half * core, half), half)
    first_q = pl.ds(pl.multiple_of(half * core, half), half // 2)
    second_q = pl.ds(pl.multiple_of(half * core + half // 2, half // 2), half // 2)
    sib_rows = pl.ds(pl.multiple_of(half * (1 - core), half), half)
    up, down = (nxt, row, col), (prv, row, col)
    beside = (seg, sib, col)
    i_ups, i_downs = (fresh(), fresh()), (fresh(), fresh())

    def outward(part, dev, i):
        return remote(w.at[:, part], wall.at[seg, :, part], dev, i)

    def onward(which, part, dev, i):
        return remote(wall.at[which, :, part], wall.at[which, :, part], dev, i)

    w_out = [
        outward(first_q, up, i_ups[0]), outward(second_q, down, i_downs[0]),
        outward(second_q, up, i_ups[1]), outward(first_q, down, i_downs[1]),
    ]
    got_prv = [onward(prv, first_q, up, i_ups[0]), onward(prv, second_q, up, i_ups[1])]
    got_nxt = [onward(nxt, second_q, down, i_downs[0]), onward(nxt, first_q, down, i_downs[1])]
    i_rup, i_rdown, i_s1, i_s2, i_s3 = fresh(), fresh(), fresh(), fresh(), fresh()
    relay_up, relay_down = onward(prv, first_q, up, i_rup), onward(nxt, second_q, down, i_rdown)
    got_rup, got_rdown = onward(far, first_q, up, i_rup), onward(far, second_q, down, i_rdown)
    share_prv, share_nxt = onward(prv, own_rows, beside, i_s1), onward(nxt, own_rows, beside, i_s2)
    share_far = onward(far, own_rows, beside, i_s3)
    got_s1, got_s2 = onward(prv, sib_rows, beside, i_s1), onward(nxt, sib_rows, beside, i_s2)
    got_s3 = onward(far, sib_rows, beside, i_s3)
    b_out, b_in = [], []
    for k in range(1, SEG):
        i = fresh()
        b_out.append(remote(b, ball.at[seg], (lax.rem(seg + k, SEG), row, col), i))
        b_in.append(remote(b, ball.at[lax.rem(seg + SEG - k, SEG)], (lax.rem(seg + k, SEG), row, col), i))

    for copy in w_out:
        copy.start()
    start_edges(x_edges[0])
    for copy in b_out:
        copy.start()
    start_edges(x_edges[1])
    start_edges(g_edges)

    def pass_near():
        got_prv[0].wait_recv()
        relay_up.start()
        got_nxt[0].wait_recv()
        relay_down.start()
        got_prv[1].wait_recv()
        share_prv.start()
        got_nxt[1].wait_recv()
        share_nxt.start()

    def pass_far():
        got_rup.wait_recv()
        got_rdown.wait_recv()
        share_far.start()

    def need(k):
        pl.when(seg == k)(mine_w.wait)
        pl.when(nxt == k)(got_s2.wait_recv)
        pl.when(far == k)(got_s3.wait_recv)
        pl.when(prv == k)(got_s1.wait_recv)

    def in_image(first, step, count):
        shape = (count, wp, chan)
        r = row * rows - REACH + first + step * lax.broadcasted_iota(jnp.int32, shape, 0)
        c = col * width - PAD + lax.broadcasted_iota(jnp.int32, shape, 1)
        return (r >= 0) & (r < nrow * rows) & (c >= 0) & (c < ncol * width)

    mask[...] = jnp.where(in_image(0, 1, tall), 1.0, 0.0).reshape(mask.shape)

    def trio(value):
        flat = value.reshape(-1, chan)
        n = flat.shape[0]
        return [
            v.astype(BF).reshape(value.shape)
            for v in (pltpu.roll(flat, 1, 0), flat, pltpu.roll(flat, n - 1, 0))
        ]

    def take_in(m):
        v = xin[m].astype(F32)[:, PAD : PAD + wp]
        v = jnp.where(mask[...].reshape(tall, wp, chan) > 0.0, v, 0.0)
        xs[m] = v.astype(BF).reshape(tall // 2, 2, wp, chan)
        for t, part in enumerate(trio(jnp.maximum(v, 0.0))):
            aa[0, m, :, :, :, pl.ds(t * chan, chan)] = part.reshape(tall // 2, 2, wp, chan)

    def wait_in(m):
        mine[m].wait()
        wait_edges(x_edges[m])

    zero = jnp.zeros((chan, chan), BF)

    def tile(k, p, q):
        return wall[k, 3 * p + q] if 0 <= p <= 2 else zero

    def there(k):
        rows_of = [
            jnp.concatenate([tile(k, a, t), tile(k, a - 1, t)], axis=1)
            for a in range(4) for t in range(3)
        ]
        return jnp.concatenate(rows_of, axis=0)

    def back(k):
        rows_of = [
            jnp.concatenate([tile(k, h + 2 - a, 2 - t) for a in range(4) for t in range(3)], axis=1)
            for h in range(2)
        ]
        return jnp.concatenate(rows_of, axis=0)

    def windows(ref, start, count):
        parts = []
        for a in range(4):
            r = start - 1 + a
            parts.append(ref[r // 2 : r // 2 + count // 2, r % 2].reshape(-1, 3 * chan))
        return jnp.concatenate(parts, axis=1)

    def chunked(multiply, finish, start, count, which):
        before = None
        for m in which:
            for c in range(0, count, CHUNK):
                now = (m, start + c, min(CHUNK, count - c))
                product = multiply(*now)
                if before:
                    finish(*before)
                before = (*now, product)
        finish(*before)

    def forward(s, which=range(MB)):
        start, count = (s + 1, tall - 2 * (s + 1)) if s < SEG - 1 else (REACH, rows)

        def multiply(m, first, n):
            return jnp.dot(windows(aa.at[s, m], first, n), there(s), preferred_element_type=F32)

        def finish(m, first, n, y):
            n = n // 2
            for h in range(2):
                i, par = (first + h) // 2, (first + h) % 2
                x = xs[m, i : i + n, par].astype(F32)
                x = x + (y[:, h * chan : (h + 1) * chan].reshape(n, wp, chan) + ball[s][None])
                x = jnp.where(mask[i : i + n, par] > 0.0, x, 0.0).astype(BF)
                xs[m, i : i + n, par] = x
                if s < SEG - 1:
                    for t, part in enumerate(trio(jnp.maximum(x.astype(F32), 0.0))):
                        aa[s + 1, m, i : i + n, par, :, pl.ds(t * chan, chan)] = part

        chunked(multiply, finish, start, count, which)

    def block_of(ref, m):
        lo, up_to = REACH // 2, hi // 2
        return ref[m, lo:up_to].reshape(rows, wp, chan).astype(F32)

    def emit_x():
        def one(m):
            ox[m] = block_of(xs, m)[:, PAD : PAD + width].astype(BF)

        both(one)

    def emit_g():
        def one(m):
            og[m] = block_of(gs, m)[:, PAD : PAD + width].astype(BF)

        both(one)

    wait_in(0)
    take_in(0)
    pass_near()
    pass_word(1)
    pl.when(seg == 2)(pass_far)
    need(0)
    mine_b.wait()
    for copy in b_in:
        copy.wait_recv()
    forward(0, (0,))
    wait_in(1)
    take_in(1)
    forward(0, (1,))
    pass_word(2)
    pl.when(seg == 3)(pass_far)
    pl.when(seg == 0)(emit_x)
    need(1)
    forward(1)
    pass_word(3)
    pl.when(seg < 2)(pass_far)
    pl.when(seg == 1)(emit_x)
    mine_g.wait()
    wait_edges(g_edges)
    edge = REACH - GREACH

    def take_in_grad(m):
        v = gin[m].astype(F32)[:, PAD : PAD + wp]
        lo, n = edge // 2, tall // 2 - edge
        v = jnp.where(mask[lo : lo + n].reshape(v.shape) > 0.0, v, 0.0)
        gs[m, lo : lo + n] = v.astype(BF).reshape(n, 2, wp, chan)
        for t, part in enumerate(trio(v)):
            gg[1, m, lo : lo + n, :, :, pl.ds(t * chan, chan)] = part.reshape(n, 2, wp, chan)
        nothing = jnp.zeros((2, wp, chan), BF)
        gm[m, 0:2] = nothing
        gm[m, rows + 2 : rows + 4] = nothing

    both(take_in_grad)
    need(2)
    forward(2)
    pass_word(4)
    pl.when(seg == 2)(emit_x)
    need(3)

    def keep():
        c = lax.broadcasted_iota(jnp.int32, (rows, wp, chan), 1)
        def one(m):
            v = jnp.where((c >= PAD) & (c < PAD + width), block_of(gs, m), 0.0)
            gm[m, 2 : rows + 2] = v.astype(BF)

        both(one)

    def backward(k, which, slot, start, count, more):
        def multiply(m, first, n):
            return lax.dot_general(
                windows(gg.at[slot, m], first, n), back(k), (((1,), (1,)), ((), ())),
                preferred_element_type=F32,
            )

        def finish(m, first, n, y):
            n = n // 2
            for h in range(2):
                i, par = (first + h) // 2, (first + h) % 2
                on = aa[k, m, i : i + n, par, :, pl.ds(chan, chan)].astype(F32) > 0.0
                g = gs[m, i : i + n, par].astype(F32)
                y_h = y[:, h * chan : (h + 1) * chan].reshape(n, wp, chan)
                g = (g + jnp.where(on, y_h, 0.0)).astype(BF)
                gs[m, i : i + n, par] = g
                if more:
                    for t, part in enumerate(trio(g.astype(F32))):
                        gg[1 - slot, m, i : i + n, par, :, pl.ds(t * chan, chan)] = part

        chunked(multiply, finish, start, count, which)

    for k in range(SEG - 1, 0, -1):

        def stage(k=k):
            backward(k, range(MB), k % 2, REACH - k, rows + 2 * k, True)

        pl.when(seg < k)(stage)
        if k == SEG - 1:
            pass_word(5)
    keep()

    def own_grad(m):
        backward(seg, (m,), lax.rem(seg, 2), REACH, rows, False)

    def last_x():
        forward(SEG - 1)
        emit_x()

    total = None
    for m in range(MB):
        lo, up_to = REACH // 2 - 1, hi // 2 + 1
        act = aa[seg, m, lo:up_to].reshape(rows + 4, wp, 3 * chan)[1 : rows + 3].reshape(-1, 3 * chan)
        grads = jnp.concatenate(
            [gm[m, 1 - p : rows + 3 - p].reshape(-1, chan) for p in (-1, 0, 1)], axis=1
        )
        term = lax.dot_general(act, grads, (((0,), (0,)), ((), ())), preferred_element_type=F32)
        total = term if total is None else total + term
    for p in range(3):
        for q in range(3):
            dw[3 * p + q] = total[q * chan : (q + 1) * chan, p * chan : (p + 1) * chan]

    def exchange(pairs):
        for copy, _ in pairs:
            copy.start()
        return pairs

    def arrived(pairs):
        for _, copy in pairs:
            copy.wait_recv()

    s_core[...] = dw[:, sib_rows].astype(BF)
    i = fresh()
    core_sum = remote(s_core, r_core, beside, i)
    core_sum.start()
    own_grad(0)
    core_sum.wait_recv()
    d_half[...] = (dw[:, own_rows] + r_core[...].astype(F32)).astype(BF)

    share = (TAPS - 1) // nz
    main = TAPS - 1
    last_tap = pl.ds(main, 1)
    cols = [wrap(col + k, ncol) for k in range(ncol)]
    zs = [wrap(z + k, nz) for k in range(nz)]
    strips = [pl.ds(pl.multiple_of(strip * c, strip), strip) for c in cols]
    places = [pl.ds(pl.multiple_of(half * core + strip * c, strip), strip) for c in cols]
    taps = [pl.ds(r * share, share) for r in zs]
    slots = [[c * nz + r for r in zs] for c in cols]
    steps = [(ky, kz) for ky in range(ncol) for kz in range(nz) if ky or kz]
    steps.sort(key=lambda s: -min(s[0], ncol - s[0]) - min(s[1], nz - s[1]))

    def device(ky, kz):
        return seg, 2 * zs[kz] + core, cols[ky]

    tap_col = [
        remote(d_half.at[last_tap, strips[k]], r_tap_col.at[k - 1], device(k, 0), fresh())
        for k in range(1, ncol)
    ]
    for copy in tap_col:
        copy.start()

    sums = []
    for ky, kz in steps:
        i = fresh()
        src = d_half.at[taps[kz], strips[ky]]
        sums.append((
            remote(src, r_main.at[slots[0][0]], device(ky, kz), i),
            remote(src, r_main.at[slots[-ky % ncol][-kz % nz]], device(ky, kz), i),
        ))
    for copy, _ in sums:
        copy.start()
    r_main[slots[0][0]] = d_half[taps[0], strips[0]]
    own_grad(1)
    emit_g()
    pl.when(seg == SEG - 1)(last_x)

    def total_of(ref, count):
        done = ref[0].astype(F32)
        for k in range(1, count):
            done = done + ref[k].astype(F32)
        return done

    for copy in tap_col:
        copy.wait_recv()
    tap = d_half[last_tap, strips[0]].astype(F32) + total_of(r_tap_col, ncol - 1)
    s_tap[...] = tap.astype(BF)
    r_tap_row[z] = tap.astype(BF)
    tap_row = []
    for k in range(1, nz):
        i = fresh()
        tap_row.append((
            remote(s_tap, r_tap_row.at[z], device(0, k), i),
            remote(s_tap, r_tap_row.at[zs[nz - k]], device(0, k), i),
        ))
    for copy, _ in tap_row:
        copy.start()

    spread = []
    for ky, kz in steps:
        i = fresh()
        src = full.at[taps[0], places[0]]
        spread.append((
            remote(src, src, device(ky, kz), i),
            remote(src, full.at[taps[-kz % nz], places[-ky % ncol]], device(ky, kz), i),
        ))
    for _, copy in reversed(sums):
        copy.wait_recv()
    full[taps[0], places[0]] = (total_of(r_main, ncol * nz) * scale).astype(BF)
    for copy, _ in spread:
        copy.start()
    for _, copy in tap_row:
        copy.wait_recv()
    full[last_tap, places[0]] = (total_of(r_tap_row, nz) * scale).astype(BF)
    tap_all = []
    for k in range(1, ncol):
        i = fresh()
        src = full.at[last_tap, places[0]]
        tap_all.append((
            remote(src, src, device(k, 0), i),
            remote(src, full.at[last_tap, places[ncol - k]], device(k, 0), i),
        ))
    for copy, _ in tap_all:
        copy.start()

    for copies in (*x_edges, g_edges):
        for copy, to, _ in copies:
            pl.when(to)(copy.wait_send)
    for copy in (*w_out, relay_up, relay_down, share_prv, share_nxt, share_far, *b_out):
        copy.wait_send()
    for copy, _ in (*sums, *tap_row):
        copy.wait_send()
    for copy in (core_sum, *tap_col):
        copy.wait_send()

    for _, copy in (*reversed(spread), *tap_all):
        copy.wait_recv()
    i = fresh()
    core_all = remote(full.at[:, own_rows], full.at[:, own_rows], beside, i)
    core_got = remote(full.at[:, own_rows], full.at[:, sib_rows], beside, i)
    core_all.start()
    for copy, _ in (*spread, *tap_all):
        copy.wait_send()
    core_got.wait_recv()
    core_all.wait_send()


def write_kernel(x, g, k, ox, og, ow, buf, sems):
    copies = [pltpu.make_async_copy(x, ox, sems.at[0]), pltpu.make_async_copy(g, og, sems.at[1])]
    for copy in copies:
        copy.start()
    buf[...] = k[...].astype(F32)
    copies.append(pltpu.make_async_copy(buf, ow, sems.at[2]))
    copies[-1].start()
    for copy in copies:
        copy.wait()


def body(images, cotangent, weights, biases):
    _, rows, width, chan = images.shape
    nrow, ncol = lax.axis_size("row"), lax.axis_size("col")
    nz = nrow // 2
    scale = 1.0 / math.sqrt(MB * rows * nrow * width * ncol)
    dims = (rows, width, chan, nrow, ncol, scale)
    tall, wp = rows + 2 * REACH, width + 2 * PAD
    wide = width + 2 * SIDE
    half, strip = chan // 2, chan // 2 // ncol
    share = (TAPS - 1) // nz
    vm = pltpu.VMEM
    chips = ncol * nz
    sems = 8 * 3 + 9 + 3 + 2 + 2 * (chips - 1) + 2 * (ncol - 1) + nz - 1
    anywhere = pl.BlockSpec(memory_space=pl.ANY)
    inside = pl.BlockSpec(memory_space=pltpu.VMEM)
    call = pl.pallas_call(
        functools.partial(body_kernel, dims),
        out_shape=(vm(images.shape, BF), vm(images.shape, BF), vm((TAPS, chan, chan), BF)),
        in_specs=[anywhere] * 4,
        out_specs=(inside,) * 3,
        scratch_shapes=[
            vm((MB, tall, wide, chan), BF),
            vm((MB, rows + 2 * GREACH, wide, chan), BF),
            vm((SEG, TAPS, chan, chan), BF),
            vm((SEG, 1, chan), F32),
            vm((SEG, MB, tall // 2, 2, wp, 3 * chan), BF),
            vm((MB, tall // 2, 2, wp, chan), BF),
            vm((2, MB, tall // 2, 2, wp, 3 * chan), BF),
            vm((MB, tall // 2, 2, wp, chan), BF),
            vm((MB, rows + 4, wp, chan), BF),
            vm((tall // 2, 2, wp, chan), F32),
            vm((TAPS, chan, chan), F32),
            vm((TAPS, half, chan), BF),
            vm((TAPS, half, chan), BF),
            vm((TAPS, half, chan), BF),
            vm((chips, share, strip, chan), BF),
            vm((ncol - 1, 1, strip, chan), BF),
            vm((1, strip, chan), BF),
            vm((nz, 1, strip, chan), BF),
            pltpu.SemaphoreType.DMA((sems,)),
            pltpu.SemaphoreType.DMA((sems,)),
            pltpu.SemaphoreType.DMA((5,)),
            pltpu.SemaphoreType.REGULAR((WORDS,)),
        ],
        compiler_params=pltpu.CompilerParams(
            collective_id=0, has_side_effects=True, vmem_limit_bytes=56 * 2**20
        ),
    )
    results = call(images, cotangent, weights.reshape(TAPS, chan, chan), biases)
    outs, grads, kernels = pl.pallas_call(
        write_kernel,
        out_shape=(
            jax.ShapeDtypeStruct(images.shape, BF),
            jax.ShapeDtypeStruct(images.shape, BF),
            jax.ShapeDtypeStruct((TAPS, chan, chan), F32),
        ),
        in_specs=[inside] * 3,
        out_specs=(anywhere,) * 3,
        scratch_shapes=[vm((TAPS, chan, chan), F32), pltpu.SemaphoreType.DMA((3,))],
        compiler_params=pltpu.CompilerParams(vmem_limit_bytes=4 * 2**20),
    )(*results)
    return outs[None], grads[None], kernels.reshape(1, 3, 3, chan, chan)


def solution(mesh):
    placed = (
        P(None, "row", "col", None),
        P(None, "row", "col", None),
        P("segment", None, None, None, None),
        P("segment", None),
    )
    return jax.shard_map(
        body,
        mesh=mesh,
        in_specs=placed,
        out_specs=(
            P("segment", None, "row", "col", None),
            P("segment", None, "row", "col", None),
            P("segment", None, None, None, None),
        ),
        check_vma=False,
    )
```

```python
import functools
import math

import jax
import jax.numpy as jnp
from jax import lax
from jax.experimental import pallas as pl
from jax.experimental.pallas import tpu as pltpu
from jax.sharding import PartitionSpec as P

MESH = pl.DeviceIdType.MESH
BF = jnp.bfloat16
F32 = jnp.float32
SEG, MB, TAPS = 4, 2, 9
REACH = 6
GREACH = 4
WORDS = 5
CHUNK = 10
SIDE = 16
PAD = 8
DIRS = ((1, 1), (1, -1), (-1, 1), (-1, -1), (1, 0), (-1, 0), (0, 1), (0, -1))


def wrap(v, n):
    return jnp.where(v >= n, v - n, v)


def body_kernel(
    dims, images, cot, w, b, ox, og, full,
    xin, gin, wall, ball, aa, xs, gg, gs, gm, mask,
    dw, s_core, r_core, d_half, r_main, r_tap_col, s_tap, r_tap_row,
    ss, rs, ls, words,
):
    rows, width, chan, nrow, ncol, scale = dims
    nz = nrow // 2
    hi = REACH + rows
    tall = rows + 2 * REACH
    wp = width + 2 * PAD
    half, strip = chan // 2, chan // 2 // ncol
    seg, row, col = lax.axis_index("segment"), lax.axis_index("row"), lax.axis_index("col")
    core, z = lax.rem(row, 2), lax.div(row, 2)
    sib = row + 1 - 2 * core

    def both(step):
        lax.fori_loop(0, MB, lambda m, carry: (step(m), carry)[1], 0)

    counter = [0]

    def fresh():
        counter[0] += 1
        return counter[0] - 1

    def remote(src, dst, dev, i, j=None):
        return pltpu.make_async_remote_copy(
            src_ref=src, dst_ref=dst, send_sem=ss.at[i], recv_sem=rs.at[i if j is None else j],
            device_id=dev, device_id_type=MESH,
        )

    barrier = pltpu.get_barrier_semaphore()

    def greet(s, r, c):
        pl.semaphore_signal(barrier, inc=1, device_id=(s, r, c), device_id_type=MESH)

    def inside(dr, dc):
        ok = jnp.bool_(True)
        if dr:
            ok = ok & (row + dr >= 0) & (row + dr < nrow)
        if dc:
            ok = ok & (col + dc >= 0) & (col + dc < ncol)
        return ok

    met = SEG - 1 + 4
    for dr, dc in DIRS:
        if dr:
            pl.when(inside(dr, dc))(functools.partial(greet, seg, row + dr, col + dc))
            met = met + inside(dr, dc).astype(jnp.int32)
    for k in range(1, SEG):
        greet(lax.rem(seg + k, SEG), row, col)
    beside_z = [lax.rem(row + 2, nrow), lax.rem(row + nrow - 2, nrow)]
    beside_y = [lax.rem(col + 1, ncol), lax.rem(col + ncol - 1, ncol)]
    for r in beside_z:
        greet(seg, r, col)
    for c in beside_y:
        greet(seg, row, c)

    mine = [
        pltpu.make_async_copy(images.at[m], xin.at[m, pl.ds(REACH, rows), pl.ds(SIDE, width)], ls.at[m])
        for m in range(MB)
    ]
    mine_g = pltpu.make_async_copy(cot, gin.at[:, pl.ds(GREACH, rows), pl.ds(SIDE, width)], ls.at[2])
    mine_w = pltpu.make_async_copy(w, wall.at[seg], ls.at[3])
    mine_b = pltpu.make_async_copy(b, ball.at[seg], ls.at[4])
    for copy in (*mine, mine_g, mine_w, mine_b):
        copy.start()

    pl.semaphore_wait(barrier, met)

    def pass_word(n):
        if n:
            pl.semaphore_wait(words.at[n - 1], 2)
        if n < nz // 2 - 1:
            for r in beside_z:
                pl.semaphore_signal(words.at[n], inc=1, device_id=(seg, r, col), device_id_type=MESH)
        elif n < WORDS:
            for c in beside_y:
                pl.semaphore_signal(words.at[n], inc=1, device_id=(seg, row, c), device_id_type=MESH)

    pass_word(0)

    def edges(source, target, reach):
        copies = []
        src_r = {1: (rows - reach, reach), -1: (0, reach), 0: (0, rows)}
        dst_r = {1: (0, reach), -1: (reach + rows, reach), 0: (reach, rows)}
        src_c = {1: (width - SIDE, SIDE), -1: (0, SIDE), 0: (0, width)}
        dst_c = {1: (0, SIDE), -1: (SIDE + width, SIDE), 0: (SIDE, width)}
        for dr, dc in DIRS:
            copies.append((
                remote(
                    source(pl.ds(*src_r[dr]), pl.ds(*src_c[dc])),
                    target(pl.ds(*dst_r[dr]), pl.ds(*dst_c[dc])),
                    (seg, row + dr, col + dc), fresh(),
                ),
                inside(dr, dc), inside(-dr, -dc),
            ))
        return copies

    def start_edges(copies):
        for copy, to, _ in copies:
            pl.when(to)(copy.start)

    def wait_edges(copies):
        for copy, _, of in reversed(copies):
            pl.when(of)(copy.wait_recv)

    x_edges = [
        edges(lambda r, c, m=m: images.at[m, r, c], lambda r, c, m=m: xin.at[m, r, c], REACH)
        for m in range(MB)
    ]
    g_edges = edges(lambda r, c: cot.at[:, r, c], lambda r, c: gin.at[:, r, c], GREACH)

    nxt, prv, far = lax.rem(seg + 1, SEG), lax.rem(seg + SEG - 1, SEG), lax.rem(seg + 2, SEG)
    own_rows = pl.ds(pl.multiple_of(half * core, half), half)
    first_q = pl.ds(pl.multiple_of(half * core, half), half // 2)
    second_q = pl.ds(pl.multiple_of(half * core + half // 2, half // 2), half // 2)
    sib_rows = pl.ds(pl.multiple_of(half * (1 - core), half), half)
    up, down = (nxt, row, col), (prv, row, col)
    beside = (seg, sib, col)
    i_ups, i_downs = (fresh(), fresh()), (fresh(), fresh())

    def outward(part, dev, i):
        return remote(w.at[:, part], wall.at[seg, :, part], dev, i)

    def onward(which, part, dev, i):
        return remote(wall.at[which, :, part], wall.at[which, :, part], dev, i)

    w_out = [
        outward(first_q, up, i_ups[0]), outward(second_q, down, i_downs[0]),
        outward(second_q, up, i_ups[1]), outward(first_q, down, i_downs[1]),
    ]
    got_prv = [onward(prv, first_q, up, i_ups[0]), onward(prv, second_q, up, i_ups[1])]
    got_nxt = [onward(nxt, second_q, down, i_downs[0]), onward(nxt, first_q, down, i_downs[1])]
    i_rup, i_rdown, i_s1, i_s2, i_s3 = fresh(), fresh(), fresh(), fresh(), fresh()
    relay_up, relay_down = onward(prv, first_q, up, i_rup), onward(nxt, second_q, down, i_rdown)
    got_rup, got_rdown = onward(far, first_q, up, i_rup), onward(far, second_q, down, i_rdown)
    share_prv, share_nxt = onward(prv, own_rows, beside, i_s1), onward(nxt, own_rows, beside, i_s2)
    share_far = onward(far, own_rows, beside, i_s3)
    got_s1, got_s2 = onward(prv, sib_rows, beside, i_s1), onward(nxt, sib_rows, beside, i_s2)
    got_s3 = onward(far, sib_rows, beside, i_s3)
    b_out, b_in = [], []
    for k in range(1, SEG):
        i = fresh()
        b_out.append(remote(b, ball.at[seg], (lax.rem(seg + k, SEG), row, col), i))
        b_in.append(remote(b, ball.at[lax.rem(seg + SEG - k, SEG)], (lax.rem(seg + k, SEG), row, col), i))

    for copy in w_out:
        copy.start()
    start_edges(x_edges[0])
    for copy in b_out:
        copy.start()
    start_edges(x_edges[1])
    start_edges(g_edges)

    def relay():
        got_prv[0].wait_recv()
        relay_up.start()
        got_nxt[0].wait_recv()
        relay_down.start()

    def pass_near():
        got_prv[1].wait_recv()
        share_prv.start()
        got_nxt[1].wait_recv()
        share_nxt.start()

    def pass_far():
        got_rup.wait_recv()
        got_rdown.wait_recv()
        share_far.start()

    def need(k):
        pl.when(seg == k)(mine_w.wait)
        pl.when(nxt == k)(got_s2.wait_recv)
        pl.when(far == k)(got_s3.wait_recv)
        pl.when(prv == k)(got_s1.wait_recv)

    def in_image(first, step, count):
        shape = (count, wp, chan)
        r = row * rows - REACH + first + step * lax.broadcasted_iota(jnp.int32, shape, 0)
        c = col * width - PAD + lax.broadcasted_iota(jnp.int32, shape, 1)
        return (r >= 0) & (r < nrow * rows) & (c >= 0) & (c < ncol * width)

    mask[...] = jnp.where(in_image(0, 1, tall), 1.0, 0.0).reshape(mask.shape)

    def trio(value):
        flat = value.reshape(-1, chan)
        n = flat.shape[0]
        return [
            v.astype(BF).reshape(value.shape)
            for v in (pltpu.roll(flat, 1, 0), flat, pltpu.roll(flat, n - 1, 0))
        ]

    def take_in(m):
        v = xin[m].astype(F32)[:, PAD : PAD + wp]
        v = jnp.where(mask[...].reshape(tall, wp, chan) > 0.0, v, 0.0)
        xs[m] = v.astype(BF).reshape(tall // 2, 2, wp, chan)
        for t, part in enumerate(trio(jnp.maximum(v, 0.0))):
            aa[0, m, :, :, :, pl.ds(t * chan, chan)] = part.reshape(tall // 2, 2, wp, chan)

    def wait_in(m):
        mine[m].wait()
        wait_edges(x_edges[m])

    zero = jnp.zeros((chan, chan), BF)

    def tile(k, p, q):
        return wall[k, 3 * p + q] if 0 <= p <= 2 else zero

    def there(k):
        rows_of = [
            jnp.concatenate([tile(k, a, t), tile(k, a - 1, t)], axis=1)
            for a in range(4) for t in range(3)
        ]
        return jnp.concatenate(rows_of, axis=0)

    def back(k):
        rows_of = [
            jnp.concatenate([tile(k, h + 2 - a, 2 - t) for a in range(4) for t in range(3)], axis=1)
            for h in range(2)
        ]
        return jnp.concatenate(rows_of, axis=0)

    def windows(ref, start, count):
        parts = []
        for a in range(4):
            r = start - 1 + a
            parts.append(ref[r // 2 : r // 2 + count // 2, r % 2].reshape(-1, 3 * chan))
        return jnp.concatenate(parts, axis=1)

    def chunked(multiply, finish, start, count, which):
        before = None
        for m in which:
            for c in range(0, count, CHUNK):
                now = (m, start + c, min(CHUNK, count - c))
                product = multiply(*now)
                if before:
                    finish(*before)
                before = (*now, product)
        finish(*before)

    def forward(s, which=range(MB)):
        start, count = (s + 1, tall - 2 * (s + 1)) if s < SEG - 1 else (REACH, rows)

        def multiply(m, first, n):
            return jnp.dot(windows(aa.at[s, m], first, n), there(s), preferred_element_type=F32)

        def finish(m, first, n, y):
            n = n // 2
            for h in range(2):
                i, par = (first + h) // 2, (first + h) % 2
                x = xs[m, i : i + n, par].astype(F32)
                x = x + (y[:, h * chan : (h + 1) * chan].reshape(n, wp, chan) + ball[s][None])
                x = jnp.where(mask[i : i + n, par] > 0.0, x, 0.0).astype(BF)
                xs[m, i : i + n, par] = x
                if s < SEG - 1:
                    for t, part in enumerate(trio(jnp.maximum(x.astype(F32), 0.0))):
                        aa[s + 1, m, i : i + n, par, :, pl.ds(t * chan, chan)] = part

        chunked(multiply, finish, start, count, which)

    def block_of(ref, m):
        lo, up_to = REACH // 2, hi // 2
        return ref[m, lo:up_to].reshape(rows, wp, chan).astype(F32)

    def emit_x():
        def one(m):
            ox[m] = block_of(xs, m)[:, PAD : PAD + width].astype(BF)

        both(one)

    def emit_g():
        def one(m):
            og[m] = block_of(gs, m)[:, PAD : PAD + width].astype(BF)

        both(one)

    relay()
    wait_in(0)
    take_in(0)
    pass_near()
    pass_word(1)
    pl.when(seg == 2)(pass_far)
    need(0)
    mine_b.wait()
    for copy in b_in:
        copy.wait_recv()
    forward(0, (0,))
    wait_in(1)
    take_in(1)
    forward(0, (1,))
    pass_word(2)
    pl.when(seg == 3)(pass_far)
    pl.when(seg == 0)(emit_x)
    need(1)
    forward(1)
    pass_word(3)
    pl.when(seg < 2)(pass_far)
    pl.when(seg == 1)(emit_x)
    mine_g.wait()
    wait_edges(g_edges)
    edge = REACH - GREACH

    def take_in_grad(m):
        v = gin[m].astype(F32)[:, PAD : PAD + wp]
        lo, n = edge // 2, tall // 2 - edge
        v = jnp.where(mask[lo : lo + n].reshape(v.shape) > 0.0, v, 0.0)
        gs[m, lo : lo + n] = v.astype(BF).reshape(n, 2, wp, chan)
        for t, part in enumerate(trio(v)):
            gg[1, m, lo : lo + n, :, :, pl.ds(t * chan, chan)] = part.reshape(n, 2, wp, chan)
        nothing = jnp.zeros((2, wp, chan), BF)
        gm[m, 0:2] = nothing
        gm[m, rows + 2 : rows + 4] = nothing

    both(take_in_grad)
    need(2)
    forward(2)
    pass_word(4)
    pl.when(seg == 2)(emit_x)
    need(3)

    def keep():
        c = lax.broadcasted_iota(jnp.int32, (rows, wp, chan), 1)
        def one(m):
            v = jnp.where((c >= PAD) & (c < PAD + width), block_of(gs, m), 0.0)
            gm[m, 2 : rows + 2] = v.astype(BF)

        both(one)

    def backward(k, which, slot, start, count, more):
        def multiply(m, first, n):
            return lax.dot_general(
                windows(gg.at[slot, m], first, n), back(k), (((1,), (1,)), ((), ())),
                preferred_element_type=F32,
            )

        def finish(m, first, n, y):
            n = n // 2
            for h in range(2):
                i, par = (first + h) // 2, (first + h) % 2
                on = aa[k, m, i : i + n, par, :, pl.ds(chan, chan)].astype(F32) > 0.0
                g = gs[m, i : i + n, par].astype(F32)
                y_h = y[:, h * chan : (h + 1) * chan].reshape(n, wp, chan)
                g = (g + jnp.where(on, y_h, 0.0)).astype(BF)
                gs[m, i : i + n, par] = g
                if more:
                    for t, part in enumerate(trio(g.astype(F32))):
                        gg[1 - slot, m, i : i + n, par, :, pl.ds(t * chan, chan)] = part

        chunked(multiply, finish, start, count, which)

    for k in range(SEG - 1, 0, -1):

        def stage(k=k):
            backward(k, range(MB), k % 2, REACH - k, rows + 2 * k, True)

        pl.when(seg < k)(stage)
        if k == SEG - 1:
            pass_word(5)
    keep()

    def own_grad(m):
        backward(seg, (m,), lax.rem(seg, 2), REACH, rows, False)

    def last_x():
        forward(SEG - 1)
        emit_x()

    total = None
    for m in range(MB):
        lo, up_to = REACH // 2 - 1, hi // 2 + 1
        act = aa[seg, m, lo:up_to].reshape(rows + 4, wp, 3 * chan)[1 : rows + 3].reshape(-1, 3 * chan)
        grads = jnp.concatenate(
            [gm[m, 1 - p : rows + 3 - p].reshape(-1, chan) for p in (-1, 0, 1)], axis=1
        )
        term = lax.dot_general(act, grads, (((0,), (0,)), ((), ())), preferred_element_type=F32)
        total = term if total is None else total + term
    for p in range(3):
        for q in range(3):
            dw[3 * p + q] = total[q * chan : (q + 1) * chan, p * chan : (p + 1) * chan]

    def exchange(pairs):
        for copy, _ in pairs:
            copy.start()
        return pairs

    def arrived(pairs):
        for _, copy in pairs:
            copy.wait_recv()

    s_core[...] = dw[:, sib_rows].astype(BF)
    i = fresh()
    core_sum = remote(s_core, r_core, beside, i)
    core_sum.start()
    own_grad(0)
    core_sum.wait_recv()
    d_half[...] = (dw[:, own_rows] + r_core[...].astype(F32)).astype(BF)

    share = (TAPS - 1) // nz
    main = TAPS - 1
    last_tap = pl.ds(main, 1)
    cols = [wrap(col + k, ncol) for k in range(ncol)]
    zs = [wrap(z + k, nz) for k in range(nz)]
    strips = [pl.ds(pl.multiple_of(strip * c, strip), strip) for c in cols]
    places = [pl.ds(pl.multiple_of(half * core + strip * c, strip), strip) for c in cols]
    taps = [pl.ds(r * share, share) for r in zs]
    slots = [[c * nz + r for r in zs] for c in cols]
    steps = [(ky, kz) for ky in range(ncol) for kz in range(nz) if ky or kz]
    steps.sort(key=lambda s: -min(s[0], ncol - s[0]) - min(s[1], nz - s[1]))

    def device(ky, kz):
        return seg, 2 * zs[kz] + core, cols[ky]

    tap_col = [
        remote(d_half.at[last_tap, strips[k]], r_tap_col.at[k - 1], device(k, 0), fresh())
        for k in range(1, ncol)
    ]
    for copy in tap_col:
        copy.start()

    sums = []
    for ky, kz in steps:
        i = fresh()
        src = d_half.at[taps[kz], strips[ky]]
        sums.append((
            remote(src, r_main.at[slots[0][0]], device(ky, kz), i),
            remote(src, r_main.at[slots[-ky % ncol][-kz % nz]], device(ky, kz), i),
        ))
    for copy, _ in sums:
        copy.start()
    r_main[slots[0][0]] = d_half[taps[0], strips[0]]
    own_grad(1)
    emit_g()
    pl.when(seg == SEG - 1)(last_x)

    def total_of(ref, count):
        done = ref[0].astype(F32)
        for k in range(1, count):
            done = done + ref[k].astype(F32)
        return done

    for copy in tap_col:
        copy.wait_recv()
    tap = d_half[last_tap, strips[0]].astype(F32) + total_of(r_tap_col, ncol - 1)
    s_tap[...] = tap.astype(BF)
    r_tap_row[z] = tap.astype(BF)
    tap_row = []
    for k in range(1, nz):
        i = fresh()
        tap_row.append((
            remote(s_tap, r_tap_row.at[z], device(0, k), i),
            remote(s_tap, r_tap_row.at[zs[nz - k]], device(0, k), i),
        ))
    for copy, _ in tap_row:
        copy.start()

    spread = []
    for ky, kz in steps:
        i = fresh()
        src = full.at[taps[0], places[0]]
        spread.append((
            remote(src, src, device(ky, kz), i),
            remote(src, full.at[taps[-kz % nz], places[-ky % ncol]], device(ky, kz), i),
        ))
    for _, copy in reversed(sums):
        copy.wait_recv()
    full[taps[0], places[0]] = (total_of(r_main, ncol * nz) * scale).astype(BF)
    for copy, _ in spread:
        copy.start()
    for _, copy in tap_row:
        copy.wait_recv()
    full[last_tap, places[0]] = (total_of(r_tap_row, nz) * scale).astype(BF)
    tap_all = []
    for k in range(1, ncol):
        i = fresh()
        src = full.at[last_tap, places[0]]
        tap_all.append((
            remote(src, src, device(k, 0), i),
            remote(src, full.at[last_tap, places[ncol - k]], device(k, 0), i),
        ))
    for copy, _ in tap_all:
        copy.start()

    for copies in (*x_edges, g_edges):
        for copy, to, _ in copies:
            pl.when(to)(copy.wait_send)
    for copy in (*w_out, relay_up, relay_down, share_prv, share_nxt, share_far, *b_out):
        copy.wait_send()
    for copy, _ in (*sums, *tap_row):
        copy.wait_send()
    for copy in (core_sum, *tap_col):
        copy.wait_send()

    for _, copy in (*reversed(spread), *tap_all):
        copy.wait_recv()
    i = fresh()
    core_all = remote(full.at[:, own_rows], full.at[:, own_rows], beside, i)
    core_got = remote(full.at[:, own_rows], full.at[:, sib_rows], beside, i)
    core_all.start()
    for copy, _ in (*spread, *tap_all):
        copy.wait_send()
    core_got.wait_recv()
    core_all.wait_send()


def write_kernel(x, g, k, ox, og, ow, buf, sems):
    copies = [pltpu.make_async_copy(x, ox, sems.at[0]), pltpu.make_async_copy(g, og, sems.at[1])]
    for copy in copies:
        copy.start()
    buf[...] = k[...].astype(F32)
    copies.append(pltpu.make_async_copy(buf, ow, sems.at[2]))
    copies[-1].start()
    for copy in copies:
        copy.wait()


def body(images, cotangent, weights, biases):
    _, rows, width, chan = images.shape
    nrow, ncol = lax.axis_size("row"), lax.axis_size("col")
    nz = nrow // 2
    scale = 1.0 / math.sqrt(MB * rows * nrow * width * ncol)
    dims = (rows, width, chan, nrow, ncol, scale)
    tall, wp = rows + 2 * REACH, width + 2 * PAD
    wide = width + 2 * SIDE
    half, strip = chan // 2, chan // 2 // ncol
    share = (TAPS - 1) // nz
    vm = pltpu.VMEM
    chips = ncol * nz
    sems = 8 * 3 + 9 + 3 + 2 + 2 * (chips - 1) + 2 * (ncol - 1) + nz - 1
    anywhere = pl.BlockSpec(memory_space=pl.ANY)
    inside = pl.BlockSpec(memory_space=pltpu.VMEM)
    call = pl.pallas_call(
        functools.partial(body_kernel, dims),
        out_shape=(vm(images.shape, BF), vm(images.shape, BF), vm((TAPS, chan, chan), BF)),
        in_specs=[anywhere] * 4,
        out_specs=(inside,) * 3,
        scratch_shapes=[
            vm((MB, tall, wide, chan), BF),
            vm((MB, rows + 2 * GREACH, wide, chan), BF),
            vm((SEG, TAPS, chan, chan), BF),
            vm((SEG, 1, chan), F32),
            vm((SEG, MB, tall // 2, 2, wp, 3 * chan), BF),
            vm((MB, tall // 2, 2, wp, chan), BF),
            vm((2, MB, tall // 2, 2, wp, 3 * chan), BF),
            vm((MB, tall // 2, 2, wp, chan), BF),
            vm((MB, rows + 4, wp, chan), BF),
            vm((tall // 2, 2, wp, chan), F32),
            vm((TAPS, chan, chan), F32),
            vm((TAPS, half, chan), BF),
            vm((TAPS, half, chan), BF),
            vm((TAPS, half, chan), BF),
            vm((chips, share, strip, chan), BF),
            vm((ncol - 1, 1, strip, chan), BF),
            vm((1, strip, chan), BF),
            vm((nz, 1, strip, chan), BF),
            pltpu.SemaphoreType.DMA((sems,)),
            pltpu.SemaphoreType.DMA((sems,)),
            pltpu.SemaphoreType.DMA((5,)),
            pltpu.SemaphoreType.REGULAR((WORDS,)),
        ],
        compiler_params=pltpu.CompilerParams(
            collective_id=0, has_side_effects=True, vmem_limit_bytes=56 * 2**20
        ),
    )
    results = call(images, cotangent, weights.reshape(TAPS, chan, chan), biases)
    outs, grads, kernels = pl.pallas_call(
        write_kernel,
        out_shape=(
            jax.ShapeDtypeStruct(images.shape, BF),
            jax.ShapeDtypeStruct(images.shape, BF),
            jax.ShapeDtypeStruct((TAPS, chan, chan), F32),
        ),
        in_specs=[inside] * 3,
        out_specs=(anywhere,) * 3,
        scratch_shapes=[vm((TAPS, chan, chan), F32), pltpu.SemaphoreType.DMA((3,))],
        compiler_params=pltpu.CompilerParams(vmem_limit_bytes=4 * 2**20),
    )(*results)
    return outs[None], grads[None], kernels.reshape(1, 3, 3, chan, chan)


def solution(mesh):
    placed = (
        P(None, "row", "col", None),
        P(None, "row", "col", None),
        P("segment", None, None, None, None),
        P("segment", None),
    )
    return jax.shard_map(
        body,
        mesh=mesh,
        in_specs=placed,
        out_specs=(
            P("segment", None, "row", "col", None),
            P("segment", None, "row", "col", None),
            P("segment", None, None, None, None),
        ),
        check_vma=False,
    )
```
